768 devices in a mesh: gx: 16 (over x, y_lo), gy: 48 (over z, y_hi, core).
Axes of the slice: x: 4, y: 8 (y_hi: 2, y_lo: 4; y = y_hi * 4 + y_lo), z: 12, core: 2. Of those that a mesh axis runs over, the one named last changes fastest.
Arguments:
- feats: bfloat16 [16, 48, 256, 128], P('gx', 'gy'), may hold values from -6 to 6
- positions: bfloat16 [16, 48, 3, 256], P('gx', 'gy'), may hold values from 0 to 1
- atom_count: int32 [16, 48], replicated, may hold values from 64 to 256, as said below
- edge_center: int32 [16, 48, 256], P('gx', 'gy'), may hold values from 0 to 255, as said below
- edge_neighbor: int32 [16, 48, 256], P('gx', 'gy'), may hold values from 0 to 2303, as said below
- edge_valid: int32 [16, 48, 256], P('gx', 'gy'), may hold values 0 or 1
- w_center: bfloat16 [128, 128], replicated, may hold values from -0.5 to 0.5
- w_neighbor: bfloat16 [128, 128], replicated, may hold values from -0.5 to 0.5
- w_radial: float32 [8, 128], replicated, may hold values from -2 to 2
- w_second: bfloat16 [128, 128], replicated, may hold values from -0.5 to 0.5
- w_env: bfloat16 [128, 384], replicated, may hold values from -0.5 to 0.5
- readout: float32 [3, 128], replicated, may hold values from -0.5 to 0.5
Outputs:
- atom_energy: float32 [16, 48, 256], P('gx', 'gy')
- forces: float32 [16, 48, 3, 256], P('gx', 'gy')
The draws below stay inside these ranges and needn't reach their ends.
Inputs may be any that keep to these rules, and one draw needn't show every extreme that they name: `atom_count`: in each row of cells that share a gx index, exactly 12 cells hold 256 atoms and every other cell holds at most 128. `edge_center`: a real atom of the edge's own cell, below its atom_count. `edge_neighbor`: s * 256 + k with k below the atom_count of the cell that s names.
All inputs are finite; a program needn't handle non-finite values. No bound on the sum of `edge_valid` on one device may be relied on, other than what follows from the above.
Results may differ from the reference program's by a relative error of at most 0.022.
Values may be sent and summed in bfloat16 or wider, within the bound.
No kernel may reach another device: no remote copies, remote signals or barrier semaphores. Data moves between devices by JAX's collectives and lax.ppermute only.
A program may use at most 32 MiB of HBM per device.

```python
import math
import jax
import jax.numpy as jnp
from jax import lax

C = 128
NBASIS = 8
ATOMS_DEV = 256
BLK_DEV = 4
EBLK = 64
EDGES_DEV = 256
N_GX = 16
N_GY = 48


def shared_counts(key):
    scores = jax.random.randint(jax.random.fold_in(key, 11), (N_GX, N_GY), 0, 1 << 20)
    scores = scores * N_GY + jnp.arange(N_GY, dtype=jnp.int32)[None, :]
    order = jnp.argsort(scores, axis=1)
    rank = jnp.argsort(order, axis=1)
    light = jax.random.randint(jax.random.fold_in(key, 12), (N_GX, N_GY), ATOMS_DEV // 4, ATOMS_DEV // 2 + 1)
    counts = jnp.where(rank < N_GY // 4, ATOMS_DEV, light)
    return counts.astype(jnp.int32)


def draw_atom_count(key, part):
    counts = shared_counts(key)
    return counts


def draw_edge_center(key, part):
    counts = shared_counts(key)
    key = jax.random.fold_in(key, 2)
    return jax.random.randint(key, (N_GX, N_GY, EDGES_DEV), 0, counts[:, :, None]).astype(jnp.int32)


def draw_edge_neighbor(key, part):
    counts = shared_counts(key)
    key = jax.random.fold_in(key, 3)
    slot_id = jax.random.randint(jax.random.fold_in(key, 1), (N_GX, N_GY, EDGES_DEV), 0, 9)
    gx_rows = jnp.arange(N_GX, dtype=jnp.int32)[:, None, None]
    gy_rows = jnp.arange(N_GY, dtype=jnp.int32)[None, :, None]
    source_x = (gx_rows + slot_id // 3 - 1) % N_GX
    source_y = (gy_rows + slot_id % 3 - 1) % N_GY
    limits = counts[source_x, source_y]
    picked = jax.random.randint(jax.random.fold_in(key, 2), (N_GX, N_GY, EDGES_DEV), 0, limits)
    return (slot_id * ATOMS_DEV + picked).astype(jnp.int32)


def touch_ends(result, rng, smallest, largest):
    extent = result.shape
    place = [jax.random.randint(jax.random.fold_in(rng, axis), (), 0, extent[axis]) for axis in range(len(extent))]
    result = result.at[tuple(place)].set(smallest)
    longest = extent.index(max(extent))
    place[longest] = (place[longest] + 1) % extent[longest]
    return result.at[tuple(place)].set(largest)


def block_levels(own_key, shape, cuts, least, high):
    def one(position, parts):
        steps = jax.random.uniform(jax.random.fold_in(jax.random.fold_in(own_key, 6), position), (parts,), jnp.float32, least / len(cuts), high / len(cuts))
        return jnp.repeat(jnp.exp(steps), shape[position] // parts).reshape((-1,) + (1,) * (len(shape) - position - 1))

    gain = one(*cuts[0])
    for cut in cuts[1:]:
        gain = gain * one(*cut)
    return gain


def normal_values(key, dims, spread, bound, cuts=(), kind=jnp.bfloat16):
    loudness = block_levels(key, dims, cuts, -0.22, 0.18) if cuts else 1.0
    array = jax.random.normal(key, dims, jnp.float32) * spread * loudness
    return jnp.minimum(jnp.maximum(array, -bound), bound).astype(kind)


def setup_inputs(seed: int = 0) -> dict:
    keys = jax.random.split(jax.random.key(seed), 13)
    return {
        "feats": normal_values(keys[0], (N_GX, N_GY, ATOMS_DEV, C), 1.0, 6.0, ((0, 16), (1, 48))),
        "positions": jnp.clip(1.0 * jax.random.uniform(keys[1], (N_GX, N_GY, 3, ATOMS_DEV), jnp.float32) ** block_levels(keys[1], (N_GX, N_GY, 3, ATOMS_DEV), ((0, 16), (1, 48)), -0.2, 0.2), 0.0, 1.0).astype(jnp.bfloat16),
        "atom_count": draw_atom_count(jax.random.fold_in(keys[12], 71), 0),
        "edge_center": draw_edge_center(jax.random.fold_in(keys[12], 71), 0),
        "edge_neighbor": draw_edge_neighbor(jax.random.fold_in(keys[12], 71), 0),
        "edge_valid": touch_ends((jax.random.randint(keys[5], (N_GX, N_GY, EDGES_DEV), 0, 4) < 3).astype(jnp.int32), jax.random.fold_in(keys[5], 1), 0, 1),
        "w_center": normal_values(keys[6], (C, C), C ** -0.5, 0.5),
        "w_neighbor": normal_values(keys[7], (C, C), C ** -0.5, 0.5),
        "w_radial": normal_values(keys[8], (NBASIS, C), NBASIS ** -0.5, 2.0, (), jnp.float32),
        "w_second": normal_values(keys[9], (C, C), C ** -0.5, 0.5),
        "w_env": normal_values(keys[10], (C, 3 * C), C ** -0.5, 0.5),
        "readout": normal_values(keys[11], (3, C), C ** -0.5, 0.5, (), jnp.float32),
    }


ROOT_THREE = math.sqrt(3.0)
ROOT_FIFTEEN = math.sqrt(15.0)
ROOT_FIVE = math.sqrt(5.0)
LEVELS = (0, 1, 1, 1, 2, 2, 2, 2, 2)

def geometry(displace):
    dist_sq = lax.optimization_barrier(jnp.sum(displace * displace, axis=0)) + 0.25
    distance = jnp.sqrt(dist_sq)
    direction = displace / distance[None, :]
    comp_x, comp_y, comp_z = (direction[0], direction[1], direction[2])
    gammas = 0.25 * 1.5 ** jnp.arange(NBASIS, dtype=jnp.float32)
    radial_basis = jnp.exp(-gammas[:, None] * dist_sq[None, :])
    harmonics = jnp.stack([jnp.ones_like(comp_x), ROOT_THREE * comp_x, ROOT_THREE * comp_y, ROOT_THREE * comp_z, ROOT_FIFTEEN * comp_x * comp_y, ROOT_FIFTEEN * comp_y * comp_z, 0.5 * ROOT_FIVE * (3.0 * comp_z * comp_z - 1.0), ROOT_FIFTEEN * comp_x * comp_z, 0.5 * ROOT_FIFTEEN * (comp_x * comp_x - comp_y * comp_y)])
    return (radial_basis, harmonics)

def local_latent(preact, w_second):
    hidden = jax.nn.silu(preact.astype(jnp.float32)).astype(jnp.bfloat16)
    return jnp.tanh(jnp.dot(hidden, w_second, preferred_element_type=jnp.float32)).astype(jnp.bfloat16)

def edge_layer(near_side, far_ghost, pos_ghost, center, neighbor, valid_int, w_radial, w_second, w_env, readout, latent_fn):
    atom_rows = near_side.shape[0]
    channels = near_side.shape[1]
    slot_id = neighbor // atom_rows
    offset = jnp.stack([slot_id // 3 - 1, slot_id % 3 - 1, jnp.zeros_like(slot_id)]).astype(jnp.float32)
    displace = pos_ghost[:, neighbor] + offset - pos_ghost[:, 4 * atom_rows + center]
    radial_basis, harmonics = geometry(displace)
    radial = lax.dot_general(radial_basis, w_radial, (((0,), (0,)), ((), ())), precision=lax.Precision.HIGHEST)
    preact = (near_side[center].astype(jnp.float32) + far_ghost[neighbor].astype(jnp.float32) + radial).astype(jnp.bfloat16)
    latent = latent_fn(preact)
    valid_mask = valid_int.astype(jnp.float32)
    env = jnp.dot(latent, w_env, preferred_element_type=jnp.float32) * valid_mask[:, None]
    env_parts = [env[:, level * channels:(level + 1) * channels] for level in range(3)]
    energy = jnp.zeros((atom_rows,), jnp.float32)
    edge_grads = []
    for comp, level in enumerate(LEVELS):
        gathered = jax.ops.segment_sum(env_parts[level] * harmonics[comp][:, None], center, num_segments=atom_rows)
        if comp == 0:
            energy = energy + lax.optimization_barrier(jnp.sum(gathered * readout[0][None, :], axis=1))
            agg_grad = jnp.broadcast_to(readout[0][None, :], gathered.shape)
        else:
            energy = energy + lax.optimization_barrier(jnp.sum(readout[level][None, :] * gathered * gathered, axis=1))
            agg_grad = 2.0 * readout[level][None, :] * gathered
        edge_grads.append(agg_grad[center])
    env_grad = []
    for level in range(3):
        summed = jnp.zeros_like(env_parts[0])
        for comp, owner in enumerate(LEVELS):
            if owner == level:
                summed = summed + edge_grads[comp] * harmonics[comp][:, None]
        env_grad.append(summed * valid_mask[:, None])
    env_grad = jnp.concatenate(env_grad, axis=1).astype(jnp.bfloat16)
    harm_grad = jnp.stack([lax.optimization_barrier(jnp.sum(edge_grads[comp] * env_parts[LEVELS[comp]], axis=1)) for comp in range(9)])
    latent_grad = lax.dot_general(env_grad, w_env, (((1,), (1,)), ((), ())), preferred_element_type=jnp.float32)
    latent32 = latent.astype(jnp.float32)
    act_grad = (latent_grad * (1.0 - latent32 * latent32)).astype(jnp.bfloat16)
    hidden_grad = lax.dot_general(act_grad, w_second, (((1,), (1,)), ((), ())), preferred_element_type=jnp.float32)
    preact32 = preact.astype(jnp.float32)
    sigmoid_pre = jax.nn.sigmoid(preact32)
    preact_grad = hidden_grad * sigmoid_pre * (1.0 + preact32 * (1.0 - sigmoid_pre))
    basis_grad = lax.dot_general(w_radial, preact_grad, (((1,), (1,)), ((), ())), precision=lax.Precision.HIGHEST)
    _, pullback = jax.vjp(geometry, displace)
    displace_grad, = pullback((basis_grad, harm_grad))
    ghost_force = jnp.zeros((3, 9 * atom_rows), jnp.float32)
    ghost_force = ghost_force.at[:, neighbor].add(-displace_grad)
    ghost_force = ghost_force.at[:, 4 * atom_rows + center].add(displace_grad)
    return (energy, ghost_force)

def reference(feats, positions, atom_count, edge_center, edge_neighbor, edge_valid, w_center, w_neighbor, w_radial, w_second, w_env, readout):
    flat_feats = feats.reshape(-1, C)
    near_all = jnp.dot(flat_feats, w_center, preferred_element_type=jnp.float32).astype(jnp.bfloat16)
    near_all = near_all.reshape(N_GX, N_GY, ATOMS_DEV, C)
    far_all = jnp.dot(flat_feats, w_neighbor, preferred_element_type=jnp.float32).astype(jnp.bfloat16)
    far_all = far_all.reshape(N_GX, N_GY, ATOMS_DEV, C)

    def per_device(device):
        gx_index = device // N_GY
        gy_index = device % N_GY
        far_rows = []
        pos_rows = []
        for first in range(3):
            for second in range(3):
                xi = (gx_index + first - 1) % N_GX
                yi = (gy_index + second - 1) % N_GY
                far_rows.append(far_all[xi, yi])
                pos_rows.append(positions[xi, yi])
        far_ghost = jnp.concatenate(far_rows, axis=0)
        pos_ghost = jnp.concatenate(pos_rows, axis=1).astype(jnp.float32)
        cell_count = atom_count[gx_index, gy_index]
        used_blocks = (cell_count * BLK_DEV + ATOMS_DEV - 1) // ATOMS_DEV
        block_id = jnp.arange(EDGES_DEV, dtype=jnp.int32) // EBLK
        valid_int = edge_valid[gx_index, gy_index] * (block_id < used_blocks).astype(jnp.int32)
        return edge_layer(near_all[gx_index, gy_index], far_ghost, pos_ghost, edge_center[gx_index, gy_index], edge_neighbor[gx_index, gy_index], valid_int, w_radial, w_second, w_env, readout, lambda preact: local_latent(preact, w_second))
    energies, ghost_forces = lax.map(per_device, jnp.arange(N_GX * N_GY, dtype=jnp.int32))
    atom_energy = energies.reshape(N_GX, N_GY, ATOMS_DEV)
    ghost_forces = ghost_forces.reshape(N_GX, N_GY, 3, 9, ATOMS_DEV)
    forces = jnp.zeros((N_GX, N_GY, 3, ATOMS_DEV), jnp.float32)
    for first in range(3):
        for second in range(3):
            forces = forces + jnp.roll(ghost_forces[:, :, :, 3 * first + second, :], (first - 1, second - 1), axis=(0, 1))
    return (atom_energy, forces)
```

```python
import math

import jax
import jax.numpy as jnp
from jax import lax
from jax.experimental import pallas as pl
from jax.experimental.pallas import tpu as pltpu
from jax.sharding import PartitionSpec as P

NBASIS = 8
EBLK = 64
POS_ROWS = 16

ROOT_THREE = math.sqrt(3.0)
ROOT_FIFTEEN = math.sqrt(15.0)
ROOT_FIVE = math.sqrt(5.0)
GAMMAS = [0.25 * 1.5**k for k in range(NBASIS)]

NN = (((1,), (0,)), ((), ()))
NT = (((1,), (1,)), ((), ()))


def mm(a, b, dims=NN):
    return lax.dot_general(a, b, dims, preferred_element_type=jnp.float32)


def turned(w):
    return w.astype(jnp.float32).T


def halves(x):
    high = x.astype(jnp.bfloat16).astype(jnp.float32)
    return high, x - high


def prepare(
    feats,
    positions,
    atom_count,
    center,
    neighbor,
    valid,
    w_center,
    w_neighbor,
    w_radial,
    w_second,
    w_env,
    readout,
    hot_nb,
    hot_c,
    same,
    near,
    aux,
    wn_t,
    w2_t,
    we_t,
    wr_t,
    wr16,
    read_b,
):
    atoms = feats.shape[2]
    edges = center.shape[2]
    gx, gy = lax.axis_index("gx"), lax.axis_index("gy")
    c_row = center[0]
    n_row = neighbor[0]
    slot = n_row // atoms
    atom = n_row - slot * atoms
    row_a = jnp.where(slot >= 3, 1, 0) + jnp.where(slot >= 6, 1, 0)
    row_b = slot - 3 * row_a
    in_a = 2 - 2 * (gx % 2)
    in_b = 2 - 2 * (gy % 2)
    place_x = jnp.where(row_a == 1, 0, jnp.where(row_a == in_a, 1, 2))
    place_y = jnp.where(row_b == 1, 0, jnp.where(row_b == in_b, 1, 2))
    local = (3 * place_y + place_x) * atoms + atom
    stacked = jnp.concatenate(
        [
            jnp.broadcast_to(local.astype(jnp.float32), (8, edges)),
            jnp.broadcast_to(c_row.astype(jnp.float32), (8, edges)),
        ],
        axis=0,
    ).T
    n_col = stacked[:, 0:1].astype(jnp.int32)
    c_col = stacked[:, 8:9].astype(jnp.int32)
    lane = lax.broadcasted_iota(jnp.int32, (edges, atoms), 1)
    for part in range(9):
        hot_nb[:, part * atoms : (part + 1) * atoms] = jnp.where(
            lane == n_col - part * atoms, 1.0, 0.0
        ).astype(jnp.bfloat16)
    c_hot = jnp.where(lane == c_col, 1.0, 0.0).astype(jnp.bfloat16)
    hot_c[...] = c_hot
    same[...] = jnp.where(c_col == c_row, 1.0, 0.0).astype(jnp.bfloat16)

    near_all = mm(feats[0, 0], w_center[...]).astype(jnp.bfloat16)
    near[...] = mm(c_hot, near_all).T
    pos16 = jnp.concatenate(
        [positions[0, 0].astype(jnp.float32), jnp.zeros((13, atoms), jnp.float32)], axis=0
    ).astype(jnp.bfloat16)
    pos_c = mm(pos16, c_hot, NT)
    used = (atom_count[gx, gy] * (edges // EBLK) + atoms - 1) // atoms
    block = lax.broadcasted_iota(jnp.int32, (1, edges), 1) // EBLK
    mask = jnp.where(block < used, valid[0], 0).astype(jnp.float32)
    aux[...] = jnp.concatenate(
        [
            (row_a - 1).astype(jnp.float32),
            (row_b - 1).astype(jnp.float32),
            jnp.zeros((1, edges), jnp.float32),
            mask,
            jnp.zeros((4, edges), jnp.float32),
            pos_c[0:8],
        ],
        axis=0,
    )

    wn_t[...] = turned(w_neighbor[...]).astype(jnp.bfloat16)
    w2_t[...] = turned(w_second[...]).astype(jnp.bfloat16)
    we_t[...] = turned(w_env[...]).astype(jnp.bfloat16)
    high, low = halves(w_radial[...])
    wr16[...] = jnp.concatenate([high, low], axis=0).astype(jnp.bfloat16)
    wr_t[...] = (
        jnp.concatenate([high, high, low, jnp.zeros_like(high)], axis=0).T.astype(jnp.bfloat16)
    )
    channels = w_center.shape[0]
    read_t = jnp.concatenate(
        [readout[...], jnp.zeros((5, channels), jnp.float32)], axis=0
    ).T
    for level in range(3):
        read_b[level] = jnp.broadcast_to(read_t[:, level : level + 1], (channels, edges))


def layer(
    slab_own,
    slab_in,
    slab_out,
    hot_nb,
    hot_c,
    same,
    near,
    aux,
    wn_t,
    w2_t,
    we_t,
    wr_t,
    wr16,
    read_b,
    w_second,
    w_env,
    energy,
    f_own,
    f_in,
    f_out,
):
    bf16, f32 = jnp.bfloat16, jnp.float32
    channels, edges = near.shape
    atoms = hot_c.shape[1]
    wide = 3 * atoms
    rows_nb = jnp.zeros((edges, channels), f32)
    pos_nb = jnp.zeros((8, edges), f32)
    for part, slab in enumerate((slab_own, slab_in, slab_out)):
        hot = hot_nb[:, part * wide : (part + 1) * wide]
        rows_nb = rows_nb + mm(hot, slab[0:wide])
        packed = slab[wide : wide + 3 * POS_ROWS].astype(f32)
        pos = jnp.concatenate([packed[8 * k : 8 * k + 8] for k in range(6)], axis=1)
        pos = jnp.concatenate([pos, jnp.zeros_like(pos)], axis=0).astype(bf16)
        pos_nb = pos_nb + mm(pos, hot, NT)[0:8]
    far = mm(wn_t[...], rows_nb.astype(bf16), NT).astype(bf16).astype(f32)

    mask = aux[3:4]
    d = pos_nb[0:3] + aux[0:3] - aux[8:11]
    dist_sq = jnp.sum(d * d, axis=0, keepdims=True) + 0.25
    inv = lax.rsqrt(dist_sq)
    dist = jnp.sqrt(dist_sq)
    u = d / dist
    ux, uy, uz = u[0:1], u[1:2], u[2:3]
    sub = lax.broadcasted_iota(jnp.int32, (NBASIS, edges), 0)
    gamma = jnp.full((NBASIS, edges), GAMMAS[0], f32)
    for k in range(1, NBASIS):
        gamma = jnp.where(sub == k, GAMMAS[k], gamma)
    basis = jnp.exp(-gamma * dist_sq)
    b_high, b_low = halves(basis)
    b32 = jnp.concatenate([b_high, b_low, b_high, jnp.zeros_like(b_high)], axis=0).astype(bf16)
    radial = mm(wr_t[...], b32)
    pre = (near[...] + far + radial).astype(bf16).astype(f32)
    sig = jax.nn.sigmoid(pre)
    latent = jnp.tanh(mm(w2_t[...], (pre * sig).astype(bf16))).astype(bf16)
    env = mm(we_t[...], latent) * mask
    harm = [
        None,
        ROOT_THREE * ux,
        ROOT_THREE * uy,
        ROOT_THREE * uz,
        ROOT_FIFTEEN * ux * uy,
        ROOT_FIFTEEN * uy * uz,
        0.5 * ROOT_FIVE * (3.0 * uz * uz - 1.0),
        ROOT_FIFTEEN * ux * uz,
        0.5 * ROOT_FIFTEEN * (ux * ux - uy * uy),
    ]
    term = jnp.sum(read_b[0] * env[0:channels], axis=0, keepdims=True)
    grads = [read_b[0] * mask]
    hg = [None] * 9
    for level, comps in ((1, (1, 2, 3)), (2, (4, 5, 6, 7, 8))):
        part = env[level * channels : (level + 1) * channels]
        twice = 2.0 * read_b[level]
        scaled = twice * part
        total = jnp.zeros((channels, edges), f32)
        for m in comps:
            gathered = mm((part * harm[m]).astype(bf16), same[...])
            hg[m] = jnp.sum(gathered * scaled, axis=0, keepdims=True)
            total = total + gathered * harm[m]
            term = term + 0.5 * harm[m] * hg[m]
        grads.append(twice * total * mask)
    env_grad = jnp.concatenate(grads, axis=0).astype(bf16)
    lat = latent.astype(f32)
    act_grad = (mm(w_env[...], env_grad) * (1.0 - lat * lat)).astype(bf16)
    pre_grad = mm(w_second[...], act_grad) * sig * (1.0 + pre * (1.0 - sig))
    p_high, p_low = halves(pre_grad)
    both = mm(wr16[...], p_high.astype(bf16)) + mm(wr16[...], p_low.astype(bf16))
    basis_grad = both[0:NBASIS] + both[NBASIS : 2 * NBASIS]
    ds = -jnp.sum(gamma * basis * basis_grad, axis=0, keepdims=True)
    gx = ROOT_THREE * hg[1] + ROOT_FIFTEEN * (uy * hg[4] + uz * hg[7] + ux * hg[8])
    gy = ROOT_THREE * hg[2] + ROOT_FIFTEEN * (ux * hg[4] + uz * hg[5] - uy * hg[8])
    gz = ROOT_THREE * hg[3] + ROOT_FIFTEEN * (uy * hg[5] + ux * hg[7]) + 3.0 * ROOT_FIVE * uz * hg[6]
    ds = ds - 0.5 * inv * inv * (gx * ux + gy * uy + gz * uz)
    g = jnp.concatenate([gx, gy, gz], axis=0)
    dg = g * inv + 2.0 * d * ds
    four_high, four_low = halves(jnp.concatenate([dg, term], axis=0))
    lines = jnp.concatenate([four_high, four_low, jnp.zeros((8, edges), f32)], axis=0).astype(bf16)
    to_c = mm(lines, hot_c[...])
    to_c = to_c[0:4] + to_c[4:8]
    energy[0] = to_c[3:4]
    for part, out in enumerate((f_own, f_in, f_out)):
        to_nb = mm(lines, hot_nb[:, part * wide : (part + 1) * wide])
        to_nb = -(to_nb[0:3] + to_nb[4:7])
        if part == 0:
            out[:, 0:atoms] = to_nb[:, 0:atoms] + to_c[0:3]
            out[:, atoms:wide] = to_nb[:, atoms:wide]
        else:
            out[...] = to_nb


def vmem(n):
    return [pl.BlockSpec(memory_space=pltpu.VMEM)] * n


def pair_in(axis):
    return [(i, i ^ 1) for i in range(lax.axis_size(axis))]


def pair_out(axis):
    count = lax.axis_size(axis)
    return [(i, (i + 1) % count if i % 2 else (i - 1) % count) for i in range(count)]


def body(
    feats,
    positions,
    atom_count,
    edge_center,
    edge_neighbor,
    edge_valid,
    w_center,
    w_neighbor,
    w_radial,
    w_second,
    w_env,
    readout,
):
    f32, bf16 = jnp.float32, jnp.bfloat16
    atoms, channels = feats.shape[2:]
    edges = edge_center.shape[2]
    half = atoms // 2
    pos = positions[0, 0]
    gap = jnp.zeros((5, half), bf16)
    pos_rows = jnp.concatenate([pos[:, :half], gap, pos[:, half:], gap], axis=0)
    own = jnp.concatenate([feats[0, 0], pos_rows], axis=0)
    x_out = lax.ppermute(own, "gx", pair_out("gx"))
    x_in = lax.ppermute(own, "gx", pair_in("gx"))

    shape = jax.ShapeDtypeStruct
    prepared = pl.pallas_call(
        prepare,
        out_shape=[
            shape((edges, 9 * atoms), bf16),
            shape((edges, atoms), bf16),
            shape((edges, edges), bf16),
            shape((channels, edges), f32),
            shape((16, edges), f32),
            shape((channels, channels), bf16),
            shape((channels, channels), bf16),
            shape((3 * channels, channels), bf16),
            shape((channels, 4 * NBASIS), bf16),
            shape((2 * NBASIS, channels), bf16),
            shape((3, channels, edges), f32),
        ],
        in_specs=vmem(2) + [pl.BlockSpec(memory_space=pltpu.SMEM)] + vmem(9),
        out_specs=vmem(11),
        name="prepare",
        cost_estimate=pl.CostEstimate(flops=100000000, bytes_accessed=3000000, transcendentals=0),
    )(
        feats,
        positions,
        atom_count,
        edge_center,
        edge_neighbor,
        edge_valid,
        w_center,
        w_neighbor,
        w_radial,
        w_second,
        w_env,
        readout,
    )

    slab = jnp.concatenate(
        [part[:atoms] for part in (own, x_in, x_out)] + [part[atoms:] for part in (own, x_in, x_out)],
        axis=0,
    )
    y_out = lax.ppermute(slab, "gy", pair_out("gy"))
    y_in = lax.ppermute(slab, "gy", pair_in("gy"))

    energy, f_own, f_in, f_out = pl.pallas_call(
        layer,
        out_shape=[shape((1, 1, edges), f32)] + [shape((3, 3 * atoms), f32)] * 3,
        in_specs=vmem(16),
        out_specs=vmem(4),
        name="layer",
    )(slab, y_in, y_out, *prepared, w_second, w_env)

    r_out = lax.ppermute(f_out, "gy", pair_out("gy"))
    r_in = lax.ppermute(f_in, "gy", pair_in("gy"))
    column = f_own + r_out + r_in
    s_out = lax.ppermute(column[:, 2 * atoms :], "gx", pair_out("gx"))
    s_in = lax.ppermute(column[:, atoms : 2 * atoms], "gx", pair_in("gx"))
    forces = column[:, :atoms] + s_out + s_in
    return (energy, forces[None, None])


def solution(mesh):
    return jax.shard_map(
        body,
        mesh=mesh,
        in_specs=(
            P("gx", "gy", None, None),
            P("gx", "gy", None, None),
            P(),
            P("gx", "gy", None),
            P("gx", "gy", None),
            P("gx", "gy", None),
            P(),
            P(),
            P(),
            P(),
            P(),
            P(),
        ),
        out_specs=(P("gx", "gy", None), P("gx", "gy", None, None)),
        check_vma=False,
    )
```

```python
import math

import jax
import jax.numpy as jnp
from jax import lax
from jax.experimental import pallas as pl
from jax.experimental.pallas import tpu as pltpu
from jax.sharding import PartitionSpec as P

NBASIS = 8
EBLK = 64
POS_ROWS = 16

ROOT_THREE = math.sqrt(3.0)
ROOT_FIFTEEN = math.sqrt(15.0)
ROOT_FIVE = math.sqrt(5.0)
GAMMAS = [0.25 * 1.5**k for k in range(NBASIS)]

NN = (((1,), (0,)), ((), ()))
NT = (((1,), (1,)), ((), ()))


def mm(a, b, dims=NN):
    return lax.dot_general(a, b, dims, preferred_element_type=jnp.float32)


def turned(w):
    return w.astype(jnp.float32).T


def halves(x):
    high = x.astype(jnp.bfloat16).astype(jnp.float32)
    return high, x - high


def prepare(
    feats,
    positions,
    atom_count,
    center,
    neighbor,
    valid,
    w_center,
    w_neighbor,
    w_radial,
    w_second,
    w_env,
    readout,
    hot_nb,
    hot_c,
    same,
    near,
    aux,
    wn_t,
    w2_t,
    we_t,
    wr_t,
    wr16,
    read_b,
    w2_copy,
    we_copy,
):
    atoms = feats.shape[2]
    edges = center.shape[2]
    gx, gy = lax.axis_index("gx"), lax.axis_index("gy")
    c_row = center[0]
    n_row = neighbor[0]
    slot = n_row // atoms
    atom = n_row - slot * atoms
    row_a = jnp.where(slot >= 3, 1, 0) + jnp.where(slot >= 6, 1, 0)
    row_b = slot - 3 * row_a
    in_a = 2 - 2 * (gx % 2)
    in_b = 2 - 2 * (gy % 2)
    place_x = jnp.where(row_a == 1, 0, jnp.where(row_a == in_a, 1, 2))
    place_y = jnp.where(row_b == 1, 0, jnp.where(row_b == in_b, 1, 2))
    local = (3 * place_y + place_x) * atoms + atom
    stacked = jnp.concatenate(
        [
            jnp.broadcast_to(local.astype(jnp.float32), (8, edges)),
            jnp.broadcast_to(c_row.astype(jnp.float32), (8, edges)),
        ],
        axis=0,
    ).T
    n_col = stacked[:, 0:1].astype(jnp.int32)
    c_col = stacked[:, 8:9].astype(jnp.int32)
    lane = lax.broadcasted_iota(jnp.int32, (edges, atoms), 1)
    for part in range(9):
        hot_nb[:, part * atoms : (part + 1) * atoms] = jnp.where(
            lane == n_col - part * atoms, 1.0, 0.0
        ).astype(jnp.bfloat16)
    c_hot = jnp.where(lane == c_col, 1.0, 0.0).astype(jnp.bfloat16)
    hot_c[...] = c_hot
    same[...] = jnp.where(c_col == c_row, 1.0, 0.0).astype(jnp.bfloat16)

    near_all = mm(feats[0, 0], w_center[...]).astype(jnp.bfloat16)
    near[...] = mm(c_hot, near_all).T
    pos16 = jnp.concatenate(
        [positions[0, 0].astype(jnp.float32), jnp.zeros((13, atoms), jnp.float32)], axis=0
    ).astype(jnp.bfloat16)
    pos_c = mm(pos16, c_hot, NT)
    used = (atom_count[gx, gy] * (edges // EBLK) + atoms - 1) // atoms
    block = lax.broadcasted_iota(jnp.int32, (1, edges), 1) // EBLK
    mask = jnp.where(block < used, valid[0], 0).astype(jnp.float32)
    aux[...] = jnp.concatenate(
        [
            (row_a - 1).astype(jnp.float32),
            (row_b - 1).astype(jnp.float32),
            jnp.zeros((1, edges), jnp.float32),
            mask,
            jnp.zeros((4, edges), jnp.float32),
            pos_c[0:8],
        ],
        axis=0,
    )

    w2_copy[...] = w_second[...]
    we_copy[...] = w_env[...]
    wn_t[...] = turned(w_neighbor[...]).astype(jnp.bfloat16)
    w2_t[...] = turned(w_second[...]).astype(jnp.bfloat16)
    we_t[...] = turned(w_env[...]).astype(jnp.bfloat16)
    high, low = halves(w_radial[...])
    wr16[...] = jnp.concatenate([high, low], axis=0).astype(jnp.bfloat16)
    wr_t[...] = (
        jnp.concatenate([high, high, low, jnp.zeros_like(high)], axis=0).T.astype(jnp.bfloat16)
    )
    channels = w_center.shape[0]
    read_t = jnp.concatenate(
        [readout[...], jnp.zeros((5, channels), jnp.float32)], axis=0
    ).T
    for level in range(3):
        read_b[level] = jnp.broadcast_to(read_t[:, level : level + 1], (channels, edges))


def layer(
    slab_own,
    slab_in,
    slab_out,
    hot_nb,
    hot_c,
    same,
    near,
    aux,
    wn_t,
    w2_t,
    we_t,
    wr_t,
    wr16,
    read_b,
    w_second,
    w_env,
    energy,
    outer,
    inner,
):
    bf16, f32 = jnp.bfloat16, jnp.float32
    channels, edges = near.shape
    atoms = hot_c.shape[1]
    wide = 3 * atoms
    rows_nb = jnp.zeros((edges, channels), f32)
    pos_nb = jnp.zeros((8, edges), f32)
    for part, slab in enumerate((slab_own, slab_in, slab_out)):
        hot = hot_nb[:, part * wide : (part + 1) * wide]
        rows_nb = rows_nb + mm(hot, slab[0:wide])
        packed = slab[wide : wide + 3 * POS_ROWS].astype(f32)
        pos = jnp.concatenate([packed[8 * k : 8 * k + 8] for k in range(6)], axis=1)
        pos = jnp.concatenate([pos, jnp.zeros_like(pos)], axis=0).astype(bf16)
        pos_nb = pos_nb + mm(pos, hot, NT)[0:8]
    far = mm(wn_t[...], rows_nb.astype(bf16), NT).astype(bf16).astype(f32)

    mask = aux[3:4]
    d = pos_nb[0:3] + aux[0:3] - aux[8:11]
    dist_sq = jnp.sum(d * d, axis=0, keepdims=True) + 0.25
    inv = lax.rsqrt(dist_sq)
    dist = jnp.sqrt(dist_sq)
    u = d / dist
    ux, uy, uz = u[0:1], u[1:2], u[2:3]
    sub = lax.broadcasted_iota(jnp.int32, (NBASIS, edges), 0)
    gamma = jnp.full((NBASIS, edges), GAMMAS[0], f32)
    for k in range(1, NBASIS):
        gamma = jnp.where(sub == k, GAMMAS[k], gamma)
    basis = jnp.exp(-gamma * dist_sq)
    b_high, b_low = halves(basis)
    b32 = jnp.concatenate([b_high, b_low, b_high, jnp.zeros_like(b_high)], axis=0).astype(bf16)
    radial = mm(wr_t[...], b32)
    pre = (near[...] + far + radial).astype(bf16).astype(f32)
    sig = jax.nn.sigmoid(pre)
    latent = jnp.tanh(mm(w2_t[...], (pre * sig).astype(bf16))).astype(bf16)
    env = mm(we_t[...], latent) * mask
    harm = [
        None,
        ROOT_THREE * ux,
        ROOT_THREE * uy,
        ROOT_THREE * uz,
        ROOT_FIFTEEN * ux * uy,
        ROOT_FIFTEEN * uy * uz,
        0.5 * ROOT_FIVE * (3.0 * uz * uz - 1.0),
        ROOT_FIFTEEN * ux * uz,
        0.5 * ROOT_FIFTEEN * (ux * ux - uy * uy),
    ]
    term = jnp.sum(read_b[0] * env[0:channels], axis=0, keepdims=True)
    grads = [read_b[0] * mask]
    hg = [None] * 9
    for level, comps in ((1, (1, 2, 3)), (2, (4, 5, 6, 7, 8))):
        part = env[level * channels : (level + 1) * channels]
        twice = 2.0 * read_b[level]
        scaled = twice * part
        total = jnp.zeros((channels, edges), f32)
        for m in comps:
            gathered = mm((part * harm[m]).astype(bf16), same[...])
            hg[m] = jnp.sum(gathered * scaled, axis=0, keepdims=True)
            total = total + gathered * harm[m]
            term = term + 0.5 * harm[m] * hg[m]
        grads.append(twice * total * mask)
    env_grad = jnp.concatenate(grads, axis=0).astype(bf16)
    lat = latent.astype(f32)
    act_grad = (mm(w_env[...], env_grad) * (1.0 - lat * lat)).astype(bf16)
    pre_grad = mm(w_second[...], act_grad) * sig * (1.0 + pre * (1.0 - sig))
    p_high, p_low = halves(pre_grad)
    both = mm(wr16[...], p_high.astype(bf16)) + mm(wr16[...], p_low.astype(bf16))
    basis_grad = both[0:NBASIS] + both[NBASIS : 2 * NBASIS]
    ds = -jnp.sum(gamma * basis * basis_grad, axis=0, keepdims=True)
    gx = ROOT_THREE * hg[1] + ROOT_FIFTEEN * (uy * hg[4] + uz * hg[7] + ux * hg[8])
    gy = ROOT_THREE * hg[2] + ROOT_FIFTEEN * (ux * hg[4] + uz * hg[5] - uy * hg[8])
    gz = ROOT_THREE * hg[3] + ROOT_FIFTEEN * (uy * hg[5] + ux * hg[7]) + 3.0 * ROOT_FIVE * uz * hg[6]
    ds = ds - 0.5 * inv * inv * (gx * ux + gy * uy + gz * uz)
    g = jnp.concatenate([gx, gy, gz], axis=0)
    dg = g * inv + 2.0 * d * ds
    four_high, four_low = halves(jnp.concatenate([dg, term], axis=0))
    lines = jnp.concatenate([four_high, four_low, jnp.zeros((8, edges), f32)], axis=0).astype(bf16)
    to_c = mm(lines, hot_c[...])
    to_c = to_c[0:4] + to_c[4:8]
    energy[0] = to_c[3:4]
    parts = []
    for part in range(3):
        to_nb = mm(lines, hot_nb[:, part * wide : (part + 1) * wide])
        to_nb = -(to_nb[0:3] + to_nb[4:7])
        parts.append([to_nb[:, k * atoms : (k + 1) * atoms] for k in range(3)])
    me = 2 * (1 - lax.axis_index("gx") % 2) + 1 - lax.axis_index("gy") % 2
    outer[me] = jnp.zeros((8, atoms), f32)
    for toward, first, second in (
        (1, parts[2][0], parts[2][1]),
        (2, parts[0][2], parts[1][2]),
        (3, parts[2][2], jnp.zeros((3, atoms), f32)),
    ):
        gap = jnp.zeros((1, atoms), f32)
        outer[me ^ toward] = jnp.concatenate([first, gap, second, gap], axis=0)
    for k, mine in enumerate((parts[0][0] + to_c[0:3], parts[1][0], parts[0][1], parts[1][1])):
        inner[k] = jnp.concatenate([mine, jnp.zeros((1, atoms), f32)], axis=0)


def pack(feats, positions, packed, pos, sems):
    atoms = feats.shape[2]
    half = atoms // 2
    move_pos = pltpu.make_async_copy(positions.at[0, 0], pos, sems.at[0])
    move_feats = pltpu.make_async_copy(feats.at[0, 0], packed.at[0:atoms], sems.at[1])
    move_pos.start()
    move_feats.start()
    move_pos.wait()
    rows = pos[...].astype(jnp.float32)
    gap = jnp.zeros((5, half), jnp.float32)
    packed[atoms : atoms + POS_ROWS] = jnp.concatenate(
        [rows[:, :half], gap, rows[:, half:], gap], axis=0
    ).astype(jnp.bfloat16)
    move_feats.wait()


def assemble(own, x_in, x_out, slab):
    atoms = own.shape[0] - POS_ROWS
    for k, part in enumerate((own, x_in, x_out)):
        slab[k * atoms : (k + 1) * atoms] = part[0:atoms]
        start = 3 * atoms + k * POS_ROWS
        slab[start : start + POS_ROWS] = part[atoms : atoms + POS_ROWS]


def regroup(arrived, inner, sent):
    far = 2 * (1 - lax.axis_index("gx") % 2) + 1 - lax.axis_index("gy") % 2
    near = 2 * (lax.axis_index("gx") % 2) + lax.axis_index("gy") % 2
    from_y = arrived[far ^ 1]
    from_x = arrived[far ^ 2]
    from_xy = arrived[far ^ 3]
    sent[near] = inner[0] + from_y[0:4] + from_x[0:4] + from_xy[0:4]
    sent[near ^ 1] = inner[1] + from_x[4:8]
    sent[near ^ 2] = inner[2] + from_y[4:8]
    sent[near ^ 3] = inner[3]


def total(arrived, forces):
    summed = arrived[0] + arrived[1] + arrived[2] + arrived[3]
    for k in range(3):
        forces[0, k] = summed[k : k + 1]


def vmem(n):
    return [pl.BlockSpec(memory_space=pltpu.VMEM)] * n


def pair_in(axis):
    return [(i, i ^ 1) for i in range(lax.axis_size(axis))]


def pair_out(axis):
    count = lax.axis_size(axis)
    return [(i, (i + 1) % count if i % 2 else (i - 1) % count) for i in range(count)]


def squares(shift):
    rows, columns = lax.axis_size("gx"), lax.axis_size("gy")
    return [
        [
            (i + shift + a) % rows * columns + (j + shift + b) % columns
            for a in range(2)
            for b in range(2)
        ]
        for i in range(0, rows, 2)
        for j in range(0, columns, 2)
    ]


def body(
    feats,
    positions,
    atom_count,
    edge_center,
    edge_neighbor,
    edge_valid,
    w_center,
    w_neighbor,
    w_radial,
    w_second,
    w_env,
    readout,
):
    f32, bf16 = jnp.float32, jnp.bfloat16
    atoms, channels = feats.shape[2:]
    edges = edge_center.shape[2]
    shape = jax.ShapeDtypeStruct
    own = pl.pallas_call(
        pack,
        out_shape=shape((atoms + POS_ROWS, channels), bf16),
        in_specs=[pl.BlockSpec(memory_space=pl.ANY)] * 2,
        out_specs=pl.BlockSpec(memory_space=pltpu.VMEM),
        scratch_shapes=[pltpu.VMEM((3, atoms), bf16), pltpu.SemaphoreType.DMA((2,))],
        name="pack",
    )(feats, positions)
    x_out = lax.ppermute(own, "gx", pair_out("gx"))
    x_in = lax.ppermute(own, "gx", pair_in("gx"))

    *prepared, w2_copy, we_copy = pl.pallas_call(
        prepare,
        out_shape=[
            shape((edges, 9 * atoms), bf16),
            shape((edges, atoms), bf16),
            shape((edges, edges), bf16),
            shape((channels, edges), f32),
            shape((16, edges), f32),
            shape((channels, channels), bf16),
            shape((channels, channels), bf16),
            shape((3 * channels, channels), bf16),
            shape((channels, 4 * NBASIS), bf16),
            shape((2 * NBASIS, channels), bf16),
            shape((3, channels, edges), f32),
            shape((channels, channels), bf16),
            shape((channels, 3 * channels), bf16),
        ],
        in_specs=vmem(2) + [pl.BlockSpec(memory_space=pltpu.SMEM)] + vmem(9),
        out_specs=vmem(13),
        name="prepare",
        cost_estimate=pl.CostEstimate(flops=100000000, bytes_accessed=3000000, transcendentals=0),
    )(
        feats,
        positions,
        atom_count,
        edge_center,
        edge_neighbor,
        edge_valid,
        w_center,
        w_neighbor,
        w_radial,
        w_second,
        w_env,
        readout,
    )

    slab = pl.pallas_call(
        assemble,
        out_shape=shape((3 * (atoms + POS_ROWS), channels), bf16),
        in_specs=vmem(3),
        out_specs=pl.BlockSpec(memory_space=pltpu.VMEM),
        name="assemble",
    )(own, x_in, x_out)
    y_out = lax.ppermute(slab, "gy", pair_out("gy"))
    y_in = lax.ppermute(slab, "gy", pair_in("gy"))

    energy, outer, inner = pl.pallas_call(
        layer,
        out_shape=[
            shape((1, 1, edges), f32),
            shape((4, 8, atoms), f32),
            shape((4, 4, atoms), f32),
        ],
        in_specs=vmem(16),
        out_specs=vmem(3),
        name="layer",
    )(slab, y_in, y_out, *prepared, w2_copy, we_copy)

    outer = lax.all_to_all(outer, ("gx", "gy"), 0, 0, axis_index_groups=squares(1))
    sent = pl.pallas_call(
        regroup,
        out_shape=shape((4, 4, atoms), f32),
        in_specs=vmem(2),
        out_specs=pl.BlockSpec(memory_space=pltpu.VMEM),
        name="regroup",
    )(outer, inner)
    sent = lax.all_to_all(sent, ("gx", "gy"), 0, 0, axis_index_groups=squares(0))
    forces = pl.pallas_call(
        total,
        out_shape=shape((1, 3, 1, atoms), f32),
        in_specs=vmem(1),
        out_specs=pl.BlockSpec(memory_space=pltpu.VMEM),
        name="total",
    )(sent)
    return (energy, jnp.swapaxes(forces, 1, 2))


def solution(mesh):
    return jax.shard_map(
        body,
        mesh=mesh,
        in_specs=(
            P("gx", "gy", None, None),
            P("gx", "gy", None, None),
            P(),
            P("gx", "gy", None),
            P("gx", "gy", None),
            P("gx", "gy", None),
            P(),
            P(),
            P(),
            P(),
            P(),
            P(),
        ),
        out_specs=(P("gx", "gy", None), P("gx", "gy", None, None)),
        check_vma=False,
    )
```

```python
import math

import jax
import jax.numpy as jnp
from jax import lax
from jax.experimental import pallas as pl
from jax.experimental.pallas import tpu as pltpu
from jax.sharding import PartitionSpec as P

NBASIS = 8
EBLK = 64
POS_ROWS = 16

ROOT_THREE = math.sqrt(3.0)
ROOT_FIFTEEN = math.sqrt(15.0)
ROOT_FIVE = math.sqrt(5.0)
GAMMAS = [0.25 * 1.5**k for k in range(NBASIS)]

NN = (((1,), (0,)), ((), ()))
NT = (((1,), (1,)), ((), ()))


def mm(a, b, dims=NN):
    return lax.dot_general(a, b, dims, preferred_element_type=jnp.float32)


def turned(w):
    return w.astype(jnp.float32).T


def halves(x):
    high = x.astype(jnp.bfloat16).astype(jnp.float32)
    return high, x - high


def prepare(
    feats,
    positions,
    atom_count,
    center,
    neighbor,
    valid,
    w_center,
    w_neighbor,
    w_radial,
    w_second,
    w_env,
    readout,
    hot_nb,
    hot_c,
    same,
    near,
    aux,
    wn_t,
    w2_t,
    we_t,
    wr_t,
    wr16,
    read_b,
    w2_copy,
    we_copy,
):
    atoms = feats.shape[2]
    edges = center.shape[2]
    gx, gy = lax.axis_index("gx"), lax.axis_index("gy")
    c_row = center[0]
    n_row = neighbor[0]
    slot = n_row // atoms
    atom = n_row - slot * atoms
    row_a = jnp.where(slot >= 3, 1, 0) + jnp.where(slot >= 6, 1, 0)
    row_b = slot - 3 * row_a
    in_a = 2 - 2 * (gx % 2)
    in_b = 2 - 2 * (gy % 2)
    place_x = jnp.where(row_a == 1, 0, jnp.where(row_a == in_a, 1, 2))
    place_y = jnp.where(row_b == 1, 0, jnp.where(row_b == in_b, 1, 2))
    local = (3 * place_y + place_x) * atoms + atom
    stacked = jnp.concatenate(
        [
            jnp.broadcast_to(local.astype(jnp.float32), (8, edges)),
            jnp.broadcast_to(c_row.astype(jnp.float32), (8, edges)),
        ],
        axis=0,
    ).T
    n_col = stacked[:, 0:1].astype(jnp.int32)
    c_col = stacked[:, 8:9].astype(jnp.int32)
    lane = lax.broadcasted_iota(jnp.int32, (edges, atoms), 1)
    for part in range(9):
        hot_nb[:, part * atoms : (part + 1) * atoms] = jnp.where(
            lane == n_col - part * atoms, 1.0, 0.0
        ).astype(jnp.bfloat16)
    c_hot = jnp.where(lane == c_col, 1.0, 0.0).astype(jnp.bfloat16)
    hot_c[...] = c_hot
    same[...] = jnp.where(c_col == c_row, 1.0, 0.0).astype(jnp.bfloat16)

    near_all = mm(feats[0, 0], w_center[...]).astype(jnp.bfloat16)
    near[...] = mm(c_hot, near_all).T
    pos16 = jnp.concatenate(
        [positions[0, 0].astype(jnp.float32), jnp.zeros((13, atoms), jnp.float32)], axis=0
    ).astype(jnp.bfloat16)
    pos_c = mm(pos16, c_hot, NT)
    used = (atom_count[gx, gy] * (edges // EBLK) + atoms - 1) // atoms
    block = lax.broadcasted_iota(jnp.int32, (1, edges), 1) // EBLK
    mask = jnp.where(block < used, valid[0], 0).astype(jnp.float32)
    aux[...] = jnp.concatenate(
        [
            (row_a - 1).astype(jnp.float32),
            (row_b - 1).astype(jnp.float32),
            jnp.zeros((1, edges), jnp.float32),
            mask,
            jnp.zeros((4, edges), jnp.float32),
            pos_c[0:8],
        ],
        axis=0,
    )

    w2_copy[...] = w_second[...]
    we_copy[...] = w_env[...]
    wn_t[...] = turned(w_neighbor[...]).astype(jnp.bfloat16)
    w2_t[...] = turned(w_second[...]).astype(jnp.bfloat16)
    we_t[...] = turned(w_env[...]).astype(jnp.bfloat16)
    high, low = halves(w_radial[...])
    wr16[...] = jnp.concatenate([high, low], axis=0).astype(jnp.bfloat16)
    wr_t[...] = (
        jnp.concatenate([high, high, low, jnp.zeros_like(high)], axis=0).T.astype(jnp.bfloat16)
    )
    channels = w_center.shape[0]
    read_t = jnp.concatenate(
        [readout[...], jnp.zeros((5, channels), jnp.float32)], axis=0
    ).T
    for level in range(3):
        read_b[level] = jnp.broadcast_to(read_t[:, level : level + 1], (channels, edges))


def layer(
    slab_own,
    slab_in,
    slab_out,
    hot_nb,
    hot_c,
    same,
    near,
    aux,
    wn_t,
    w2_t,
    we_t,
    wr_t,
    wr16,
    read_b,
    w_second,
    w_env,
    energy,
    f_own,
    f_in,
    f_out,
):
    bf16, f32 = jnp.bfloat16, jnp.float32
    channels, edges = near.shape
    atoms = hot_c.shape[1]
    wide = 3 * atoms
    rows_nb = jnp.zeros((edges, channels), f32)
    pos_nb = jnp.zeros((8, edges), f32)
    for part, slab in enumerate((slab_own, slab_in, slab_out)):
        hot = hot_nb[:, part * wide : (part + 1) * wide]
        rows_nb = rows_nb + mm(hot, slab[0:wide])
        packed = slab[wide : wide + 3 * POS_ROWS].astype(f32)
        pos = jnp.concatenate([packed[8 * k : 8 * k + 8] for k in range(6)], axis=1)
        pos = jnp.concatenate([pos, jnp.zeros_like(pos)], axis=0).astype(bf16)
        pos_nb = pos_nb + mm(pos, hot, NT)[0:8]
    far = mm(wn_t[...], rows_nb.astype(bf16), NT).astype(bf16).astype(f32)

    mask = aux[3:4]
    d = pos_nb[0:3] + aux[0:3] - aux[8:11]
    dist_sq = jnp.sum(d * d, axis=0, keepdims=True) + 0.25
    inv = lax.rsqrt(dist_sq)
    dist = jnp.sqrt(dist_sq)
    u = d / dist
    ux, uy, uz = u[0:1], u[1:2], u[2:3]
    sub = lax.broadcasted_iota(jnp.int32, (NBASIS, edges), 0)
    gamma = jnp.full((NBASIS, edges), GAMMAS[0], f32)
    for k in range(1, NBASIS):
        gamma = jnp.where(sub == k, GAMMAS[k], gamma)
    basis = jnp.exp(-gamma * dist_sq)
    b_high, b_low = halves(basis)
    b32 = jnp.concatenate([b_high, b_low, b_high, jnp.zeros_like(b_high)], axis=0).astype(bf16)
    radial = mm(wr_t[...], b32)
    pre = (near[...] + far + radial).astype(bf16).astype(f32)
    sig = jax.nn.sigmoid(pre)
    latent = jnp.tanh(mm(w2_t[...], (pre * sig).astype(bf16))).astype(bf16)
    env = mm(we_t[...], latent) * mask
    harm = [
        None,
        ROOT_THREE * ux,
        ROOT_THREE * uy,
        ROOT_THREE * uz,
        ROOT_FIFTEEN * ux * uy,
        ROOT_FIFTEEN * uy * uz,
        0.5 * ROOT_FIVE * (3.0 * uz * uz - 1.0),
        ROOT_FIFTEEN * ux * uz,
        0.5 * ROOT_FIFTEEN * (ux * ux - uy * uy),
    ]
    term = jnp.sum(read_b[0] * env[0:channels], axis=0, keepdims=True)
    grads = [read_b[0] * mask]
    hg = [None] * 9
    for level, comps in ((1, (1, 2, 3)), (2, (4, 5, 6, 7, 8))):
        part = env[level * channels : (level + 1) * channels]
        twice = 2.0 * read_b[level]
        scaled = twice * part
        total = jnp.zeros((channels, edges), f32)
        for m in comps:
            gathered = mm((part * harm[m]).astype(bf16), same[...])
            hg[m] = jnp.sum(gathered * scaled, axis=0, keepdims=True)
            total = total + gathered * harm[m]
            term = term + 0.5 * harm[m] * hg[m]
        grads.append(twice * total * mask)
    env_grad = jnp.concatenate(grads, axis=0).astype(bf16)
    lat = latent.astype(f32)
    act_grad = (mm(w_env[...], env_grad) * (1.0 - lat * lat)).astype(bf16)
    pre_grad = mm(w_second[...], act_grad) * sig * (1.0 + pre * (1.0 - sig))
    p_high, p_low = halves(pre_grad)
    both = mm(wr16[...], p_high.astype(bf16)) + mm(wr16[...], p_low.astype(bf16))
    basis_grad = both[0:NBASIS] + both[NBASIS : 2 * NBASIS]
    ds = -jnp.sum(gamma * basis * basis_grad, axis=0, keepdims=True)
    gx = ROOT_THREE * hg[1] + ROOT_FIFTEEN * (uy * hg[4] + uz * hg[7] + ux * hg[8])
    gy = ROOT_THREE * hg[2] + ROOT_FIFTEEN * (ux * hg[4] + uz * hg[5] - uy * hg[8])
    gz = ROOT_THREE * hg[3] + ROOT_FIFTEEN * (uy * hg[5] + ux * hg[7]) + 3.0 * ROOT_FIVE * uz * hg[6]
    ds = ds - 0.5 * inv * inv * (gx * ux + gy * uy + gz * uz)
    g = jnp.concatenate([gx, gy, gz], axis=0)
    dg = g * inv + 2.0 * d * ds
    four_high, four_low = halves(jnp.concatenate([dg, term], axis=0))
    lines = jnp.concatenate([four_high, four_low, jnp.zeros((8, edges), f32)], axis=0).astype(bf16)
    to_c = mm(lines, hot_c[...])
    to_c = to_c[0:4] + to_c[4:8]
    energy[0] = to_c[3:4]
    for part, out in enumerate((f_own, f_in, f_out)):
        to_nb = mm(lines, hot_nb[:, part * wide : (part + 1) * wide])
        to_nb = -(to_nb[0:3] + to_nb[4:7])
        if part == 0:
            out[:, 0:atoms] = to_nb[:, 0:atoms] + to_c[0:3]
            out[:, atoms:wide] = to_nb[:, atoms:wide]
        else:
            out[...] = to_nb


def pack(feats, positions, packed, pos, sems):
    atoms = feats.shape[2]
    half = atoms // 2
    move_pos = pltpu.make_async_copy(positions.at[0, 0], pos, sems.at[0])
    move_feats = pltpu.make_async_copy(feats.at[0, 0], packed.at[0:atoms], sems.at[1])
    move_pos.start()
    move_feats.start()
    move_pos.wait()
    rows = pos[...].astype(jnp.float32)
    gap = jnp.zeros((5, half), jnp.float32)
    packed[atoms : atoms + POS_ROWS] = jnp.concatenate(
        [rows[:, :half], gap, rows[:, half:], gap], axis=0
    ).astype(jnp.bfloat16)
    move_feats.wait()


def assemble(own, x_in, x_out, slab):
    atoms = own.shape[0] - POS_ROWS
    for k, part in enumerate((own, x_in, x_out)):
        slab[k * atoms : (k + 1) * atoms] = part[0:atoms]
        start = 3 * atoms + k * POS_ROWS
        slab[start : start + POS_ROWS] = part[atoms : atoms + POS_ROWS]


def grant(mib):
    return pltpu.CompilerParams(vmem_limit_bytes=mib << 20)


def vmem(n):
    return [pl.BlockSpec(memory_space=pltpu.VMEM)] * n


def pair_in(axis):
    return [(i, i ^ 1) for i in range(lax.axis_size(axis))]


def pair_out(axis):
    count = lax.axis_size(axis)
    return [(i, (i + 1) % count if i % 2 else (i - 1) % count) for i in range(count)]


def body(
    feats,
    positions,
    atom_count,
    edge_center,
    edge_neighbor,
    edge_valid,
    w_center,
    w_neighbor,
    w_radial,
    w_second,
    w_env,
    readout,
):
    f32, bf16 = jnp.float32, jnp.bfloat16
    atoms, channels = feats.shape[2:]
    edges = edge_center.shape[2]
    shape = jax.ShapeDtypeStruct
    own = pl.pallas_call(
        pack,
        out_shape=shape((atoms + POS_ROWS, channels), bf16),
        in_specs=[pl.BlockSpec(memory_space=pl.ANY)] * 2,
        out_specs=pl.BlockSpec(memory_space=pltpu.VMEM),
        scratch_shapes=[pltpu.VMEM((3, atoms), bf16), pltpu.SemaphoreType.DMA((2,))],
        name="pack",
        compiler_params=grant(2),
    )(feats, positions)
    x_out = lax.ppermute(own, "gx", pair_out("gx"))
    x_in = lax.ppermute(own, "gx", pair_in("gx"))

    *prepared, w2_copy, we_copy = pl.pallas_call(
        prepare,
        out_shape=[
            shape((edges, 9 * atoms), bf16),
            shape((edges, atoms), bf16),
            shape((edges, edges), bf16),
            shape((channels, edges), f32),
            shape((16, edges), f32),
            shape((channels, channels), bf16),
            shape((channels, channels), bf16),
            shape((3 * channels, channels), bf16),
            shape((channels, 4 * NBASIS), bf16),
            shape((2 * NBASIS, channels), bf16),
            shape((3, channels, edges), f32),
            shape((channels, channels), bf16),
            shape((channels, 3 * channels), bf16),
        ],
        in_specs=vmem(2) + [pl.BlockSpec(memory_space=pltpu.SMEM)] + vmem(9),
        out_specs=vmem(13),
        name="prepare",
        compiler_params=grant(8),
        cost_estimate=pl.CostEstimate(flops=100000000, bytes_accessed=3000000, transcendentals=0),
    )(
        feats,
        positions,
        atom_count,
        edge_center,
        edge_neighbor,
        edge_valid,
        w_center,
        w_neighbor,
        w_radial,
        w_second,
        w_env,
        readout,
    )

    slab = pl.pallas_call(
        assemble,
        out_shape=shape((3 * (atoms + POS_ROWS), channels), bf16),
        in_specs=vmem(3),
        out_specs=pl.BlockSpec(memory_space=pltpu.VMEM),
        name="assemble",
        compiler_params=grant(2),
    )(own, x_in, x_out)
    y_out = lax.ppermute(slab, "gy", pair_out("gy"))
    y_in = lax.ppermute(slab, "gy", pair_in("gy"))

    energy, f_own, f_in, f_out = pl.pallas_call(
        layer,
        out_shape=[shape((1, 1, edges), f32)] + [shape((3, 3 * atoms), f32)] * 3,
        in_specs=vmem(16),
        out_specs=vmem(4),
        name="layer",
        compiler_params=grant(8),
    )(slab, y_in, y_out, *prepared, w2_copy, we_copy)

    r_out = lax.ppermute(f_out, "gy", pair_out("gy"))
    r_in = lax.ppermute(f_in, "gy", pair_in("gy"))
    column = f_own + r_out + r_in
    s_out = lax.ppermute(column[:, 2 * atoms :], "gx", pair_out("gx"))
    s_in = lax.ppermute(column[:, atoms : 2 * atoms], "gx", pair_in("gx"))
    forces = column[:, :atoms] + s_out + s_in
    return (energy, forces[None, None])


def solution(mesh):
    return jax.shard_map(
        body,
        mesh=mesh,
        in_specs=(
            P("gx", "gy", None, None),
            P("gx", "gy", None, None),
            P(),
            P("gx", "gy", None),
            P("gx", "gy", None),
            P("gx", "gy", None),
            P(),
            P(),
            P(),
            P(),
            P(),
            P(),
        ),
        out_specs=(P("gx", "gy", None), P("gx", "gy", None, None)),
        check_vma=False,
    )
```

```python
import math

import jax
import jax.numpy as jnp
from jax import lax
from jax.experimental import pallas as pl
from jax.experimental.pallas import tpu as pltpu
from jax.sharding import PartitionSpec as P

NBASIS = 8
EBLK = 64
POS_ROWS = 16

ROOT_THREE = math.sqrt(3.0)
ROOT_FIFTEEN = math.sqrt(15.0)
ROOT_FIVE = math.sqrt(5.0)
GAMMAS = [0.25 * 1.5**k for k in range(NBASIS)]

NN = (((1,), (0,)), ((), ()))
NT = (((1,), (1,)), ((), ()))


def mm(a, b, dims=NN):
    return lax.dot_general(a, b, dims, preferred_element_type=jnp.float32)


def turned(w):
    return w.astype(jnp.float32).T


def halves(x):
    high = x.astype(jnp.bfloat16).astype(jnp.float32)
    return high, x - high


def prepare(
    feats_hbm,
    positions_hbm,
    count_hbm,
    center_hbm,
    neighbor_hbm,
    valid_hbm,
    w_center_hbm,
    w_neighbor_hbm,
    w_radial_hbm,
    w_second_hbm,
    w_env_hbm,
    readout_hbm,
    hot_nb,
    hot_c,
    same,
    near,
    aux,
    wn_t,
    w2_t,
    we_t,
    wr_t,
    wr16,
    read_b,
    w2_copy,
    we_copy,
    feats,
    positions,
    atom_count,
    center,
    neighbor,
    valid,
    w_center,
    w_neighbor,
    w_radial,
    readout,
    sems,
):
    moves = [
        pltpu.make_async_copy(source, target, sems.at[k])
        for k, (source, target) in enumerate(
            (
                (neighbor_hbm, neighbor),
                (center_hbm, center),
                (valid_hbm, valid),
                (count_hbm, atom_count),
                (feats_hbm, feats),
                (positions_hbm, positions),
                (w_center_hbm, w_center),
                (w_neighbor_hbm, w_neighbor),
                (w_second_hbm, w2_copy),
                (w_env_hbm, we_copy),
                (w_radial_hbm, w_radial),
                (readout_hbm, readout),
            )
        )
    ]
    for move in moves:
        move.start()
    atoms = feats.shape[2]
    edges = center.shape[2]
    gx, gy = lax.axis_index("gx"), lax.axis_index("gy")
    for move in moves[:4]:
        move.wait()
    c_row = center[0]
    n_row = neighbor[0]
    slot = n_row // atoms
    atom = n_row - slot * atoms
    row_a = jnp.where(slot >= 3, 1, 0) + jnp.where(slot >= 6, 1, 0)
    row_b = slot - 3 * row_a
    in_a = 2 - 2 * (gx % 2)
    in_b = 2 - 2 * (gy % 2)
    place_x = jnp.where(row_a == 1, 0, jnp.where(row_a == in_a, 1, 2))
    place_y = jnp.where(row_b == 1, 0, jnp.where(row_b == in_b, 1, 2))
    local = (3 * place_y + place_x) * atoms + atom
    stacked = jnp.concatenate(
        [
            jnp.broadcast_to(local.astype(jnp.float32), (8, edges)),
            jnp.broadcast_to(c_row.astype(jnp.float32), (8, edges)),
        ],
        axis=0,
    ).T
    n_col = stacked[:, 0:1].astype(jnp.int32)
    c_col = stacked[:, 8:9].astype(jnp.int32)
    lane = lax.broadcasted_iota(jnp.int32, (edges, atoms), 1)
    for part in range(9):
        hot_nb[:, part * atoms : (part + 1) * atoms] = jnp.where(
            lane == n_col - part * atoms, 1.0, 0.0
        ).astype(jnp.bfloat16)
    c_hot = jnp.where(lane == c_col, 1.0, 0.0).astype(jnp.bfloat16)
    hot_c[...] = c_hot
    same[...] = jnp.where(c_col == c_row, 1.0, 0.0).astype(jnp.bfloat16)

    for move in moves[4:]:
        move.wait()
    near_all = mm(feats[0, 0], w_center[...]).astype(jnp.bfloat16)
    near[...] = mm(c_hot, near_all).T
    pos16 = jnp.concatenate(
        [positions[0, 0].astype(jnp.float32), jnp.zeros((13, atoms), jnp.float32)], axis=0
    ).astype(jnp.bfloat16)
    pos_c = mm(pos16, c_hot, NT)
    here = (lax.broadcasted_iota(jnp.int32, atom_count.shape, 0) == gx) & (
        lax.broadcasted_iota(jnp.int32, atom_count.shape, 1) == gy
    )
    count = jnp.where(here, atom_count[...], 0).astype(jnp.float32)
    count = jnp.sum(jnp.sum(count, axis=1, keepdims=True), axis=0, keepdims=True)
    used = (count.astype(jnp.int32) * (edges // EBLK) + atoms - 1) // atoms
    block = lax.broadcasted_iota(jnp.int32, (1, edges), 1) // EBLK
    mask = jnp.where(block < used, valid[0], 0).astype(jnp.float32)
    aux[...] = jnp.concatenate(
        [
            (row_a - 1).astype(jnp.float32),
            (row_b - 1).astype(jnp.float32),
            jnp.zeros((1, edges), jnp.float32),
            mask,
            jnp.zeros((4, edges), jnp.float32),
            pos_c[0:8],
        ],
        axis=0,
    )

    wn_t[...] = turned(w_neighbor[...]).astype(jnp.bfloat16)
    w2_t[...] = turned(w2_copy[...]).astype(jnp.bfloat16)
    we_t[...] = turned(we_copy[...]).astype(jnp.bfloat16)
    high, low = halves(w_radial[...])
    wr16[...] = jnp.concatenate([high, low], axis=0).astype(jnp.bfloat16)
    wr_t[...] = (
        jnp.concatenate([high, high, low, jnp.zeros_like(high)], axis=0).T.astype(jnp.bfloat16)
    )
    channels = w_center.shape[0]
    read_t = jnp.concatenate(
        [readout[...], jnp.zeros((5, channels), jnp.float32)], axis=0
    ).T
    for level in range(3):
        read_b[level] = jnp.broadcast_to(read_t[:, level : level + 1], (channels, edges))


def layer(
    slab_own,
    slab_in,
    slab_out,
    hot_nb,
    hot_c,
    same,
    near,
    aux,
    wn_t,
    w2_t,
    we_t,
    wr_t,
    wr16,
    read_b,
    w_second,
    w_env,
    energy,
    f_own,
    f_in,
    f_out,
):
    bf16, f32 = jnp.bfloat16, jnp.float32
    channels, edges = near.shape
    atoms = hot_c.shape[1]
    wide = 3 * atoms
    rows_nb = jnp.zeros((edges, channels), f32)
    pos_nb = jnp.zeros((8, edges), f32)
    for part, slab in enumerate((slab_own, slab_in, slab_out)):
        hot = hot_nb[:, part * wide : (part + 1) * wide]
        rows_nb = rows_nb + mm(hot, slab[0:wide])
        packed = slab[wide : wide + 3 * POS_ROWS].astype(f32)
        pos = jnp.concatenate([packed[8 * k : 8 * k + 8] for k in range(6)], axis=1)
        pos = jnp.concatenate([pos, jnp.zeros_like(pos)], axis=0).astype(bf16)
        pos_nb = pos_nb + mm(pos, hot, NT)[0:8]
    far = mm(wn_t[...], rows_nb.astype(bf16), NT).astype(bf16).astype(f32)

    mask = aux[3:4]
    d = pos_nb[0:3] + aux[0:3] - aux[8:11]
    dist_sq = jnp.sum(d * d, axis=0, keepdims=True) + 0.25
    inv = lax.rsqrt(dist_sq)
    dist = jnp.sqrt(dist_sq)
    u = d / dist
    ux, uy, uz = u[0:1], u[1:2], u[2:3]
    sub = lax.broadcasted_iota(jnp.int32, (NBASIS, edges), 0)
    gamma = jnp.full((NBASIS, edges), GAMMAS[0], f32)
    for k in range(1, NBASIS):
        gamma = jnp.where(sub == k, GAMMAS[k], gamma)
    basis = jnp.exp(-gamma * dist_sq)
    b_high, b_low = halves(basis)
    b32 = jnp.concatenate([b_high, b_low, b_high, jnp.zeros_like(b_high)], axis=0).astype(bf16)
    radial = mm(wr_t[...], b32)
    pre = (near[...] + far + radial).astype(bf16).astype(f32)
    sig = jax.nn.sigmoid(pre)
    latent = jnp.tanh(mm(w2_t[...], (pre * sig).astype(bf16))).astype(bf16)
    env = mm(we_t[...], latent) * mask
    harm = [
        None,
        ROOT_THREE * ux,
        ROOT_THREE * uy,
        ROOT_THREE * uz,
        ROOT_FIFTEEN * ux * uy,
        ROOT_FIFTEEN * uy * uz,
        0.5 * ROOT_FIVE * (3.0 * uz * uz - 1.0),
        ROOT_FIFTEEN * ux * uz,
        0.5 * ROOT_FIFTEEN * (ux * ux - uy * uy),
    ]
    term = jnp.sum(read_b[0] * env[0:channels], axis=0, keepdims=True)
    grads = [read_b[0] * mask]
    hg = [None] * 9
    for level, comps in ((1, (1, 2, 3)), (2, (4, 5, 6, 7, 8))):
        part = env[level * channels : (level + 1) * channels]
        twice = 2.0 * read_b[level]
        scaled = twice * part
        total = jnp.zeros((channels, edges), f32)
        for m in comps:
            gathered = mm((part * harm[m]).astype(bf16), same[...])
            hg[m] = jnp.sum(gathered * scaled, axis=0, keepdims=True)
            total = total + gathered * harm[m]
            term = term + 0.5 * harm[m] * hg[m]
        grads.append(twice * total * mask)
    env_grad = jnp.concatenate(grads, axis=0).astype(bf16)
    lat = latent.astype(f32)
    act_grad = (mm(w_env[...], env_grad) * (1.0 - lat * lat)).astype(bf16)
    pre_grad = mm(w_second[...], act_grad) * sig * (1.0 + pre * (1.0 - sig))
    p_high, p_low = halves(pre_grad)
    both = mm(wr16[...], p_high.astype(bf16)) + mm(wr16[...], p_low.astype(bf16))
    basis_grad = both[0:NBASIS] + both[NBASIS : 2 * NBASIS]
    ds = -jnp.sum(gamma * basis * basis_grad, axis=0, keepdims=True)
    gx = ROOT_THREE * hg[1] + ROOT_FIFTEEN * (uy * hg[4] + uz * hg[7] + ux * hg[8])
    gy = ROOT_THREE * hg[2] + ROOT_FIFTEEN * (ux * hg[4] + uz * hg[5] - uy * hg[8])
    gz = ROOT_THREE * hg[3] + ROOT_FIFTEEN * (uy * hg[5] + ux * hg[7]) + 3.0 * ROOT_FIVE * uz * hg[6]
    ds = ds - 0.5 * inv * inv * (gx * ux + gy * uy + gz * uz)
    g = jnp.concatenate([gx, gy, gz], axis=0)
    dg = g * inv + 2.0 * d * ds
    four_high, four_low = halves(jnp.concatenate([dg, term], axis=0))
    lines = jnp.concatenate([four_high, four_low, jnp.zeros((8, edges), f32)], axis=0).astype(bf16)
    to_c = mm(lines, hot_c[...])
    to_c = to_c[0:4] + to_c[4:8]
    energy[0] = to_c[3:4]
    for part, out in enumerate((f_own, f_in, f_out)):
        to_nb = mm(lines, hot_nb[:, part * wide : (part + 1) * wide])
        to_nb = -(to_nb[0:3] + to_nb[4:7])
        if part == 0:
            out[:, 0:atoms] = to_nb[:, 0:atoms] + to_c[0:3]
            out[:, atoms:wide] = to_nb[:, atoms:wide]
        else:
            out[...] = to_nb


def pack(feats, positions, packed, pos, sems):
    atoms = feats.shape[2]
    half = atoms // 2
    move_pos = pltpu.make_async_copy(positions.at[0, 0], pos, sems.at[0])
    move_feats = pltpu.make_async_copy(feats.at[0, 0], packed.at[0:atoms], sems.at[1])
    move_pos.start()
    move_feats.start()
    move_pos.wait()
    rows = pos[...].astype(jnp.float32)
    gap = jnp.zeros((5, half), jnp.float32)
    packed[atoms : atoms + POS_ROWS] = jnp.concatenate(
        [rows[:, :half], gap, rows[:, half:], gap], axis=0
    ).astype(jnp.bfloat16)
    move_feats.wait()


def assemble(own, x_in, x_out, slab):
    atoms = own.shape[0] - POS_ROWS
    for k, part in enumerate((own, x_in, x_out)):
        slab[k * atoms : (k + 1) * atoms] = part[0:atoms]
        start = 3 * atoms + k * POS_ROWS
        slab[start : start + POS_ROWS] = part[atoms : atoms + POS_ROWS]


def grant(mib):
    return pltpu.CompilerParams(vmem_limit_bytes=mib << 20)


def vmem(n):
    return [pl.BlockSpec(memory_space=pltpu.VMEM)] * n


def in_hbm(*arrays):
    return [pltpu.with_memory_space_constraint(a, pltpu.HBM) for a in arrays]


def hbm(n):
    return [pl.BlockSpec(memory_space=pltpu.HBM)] * n


def pair_in(axis):
    return [(i, i ^ 1) for i in range(lax.axis_size(axis))]


def pair_out(axis):
    count = lax.axis_size(axis)
    return [(i, (i + 1) % count if i % 2 else (i - 1) % count) for i in range(count)]


def body(
    feats,
    positions,
    atom_count,
    edge_center,
    edge_neighbor,
    edge_valid,
    w_center,
    w_neighbor,
    w_radial,
    w_second,
    w_env,
    readout,
):
    f32, bf16 = jnp.float32, jnp.bfloat16
    atoms, channels = feats.shape[2:]
    edges = edge_center.shape[2]
    shape = jax.ShapeDtypeStruct
    own = pl.pallas_call(
        pack,
        out_shape=shape((atoms + POS_ROWS, channels), bf16),
        in_specs=hbm(2),
        out_specs=pl.BlockSpec(memory_space=pltpu.VMEM),
        scratch_shapes=[pltpu.VMEM((3, atoms), bf16), pltpu.SemaphoreType.DMA((2,))],
        name="pack",
        compiler_params=grant(2),
    )(*in_hbm(feats, positions))
    x_out = lax.ppermute(own, "gx", pair_out("gx"))
    x_in = lax.ppermute(own, "gx", pair_in("gx"))

    *prepared, w2_copy, we_copy = pl.pallas_call(
        prepare,
        out_shape=[
            shape((edges, 9 * atoms), bf16),
            shape((edges, atoms), bf16),
            shape((edges, edges), bf16),
            shape((channels, edges), f32),
            shape((16, edges), f32),
            shape((channels, channels), bf16),
            shape((channels, channels), bf16),
            shape((3 * channels, channels), bf16),
            shape((channels, 4 * NBASIS), bf16),
            shape((2 * NBASIS, channels), bf16),
            shape((3, channels, edges), f32),
            shape((channels, channels), bf16),
            shape((channels, 3 * channels), bf16),
        ],
        in_specs=hbm(12),
        out_specs=vmem(13),
        scratch_shapes=[
            pltpu.VMEM(part.shape, part.dtype)
            for part in (
                feats,
                positions,
                atom_count,
                edge_center,
                edge_neighbor,
                edge_valid,
                w_center,
                w_neighbor,
                w_radial,
                readout,
            )
        ]
        + [pltpu.SemaphoreType.DMA((12,))],
        name="prepare",
        compiler_params=grant(8),
        cost_estimate=pl.CostEstimate(flops=100000000, bytes_accessed=3000000, transcendentals=0),
    )(
        *in_hbm(
            feats,
            positions,
            atom_count,
            edge_center,
            edge_neighbor,
            edge_valid,
            w_center,
            w_neighbor,
            w_radial,
            w_second,
            w_env,
            readout,
        )
    )

    slab = pl.pallas_call(
        assemble,
        out_shape=shape((3 * (atoms + POS_ROWS), channels), bf16),
        in_specs=vmem(3),
        out_specs=pl.BlockSpec(memory_space=pltpu.VMEM),
        name="assemble",
        compiler_params=grant(2),
    )(own, x_in, x_out)
    y_out = lax.ppermute(slab, "gy", pair_out("gy"))
    y_in = lax.ppermute(slab, "gy", pair_in("gy"))

    energy, f_own, f_in, f_out = pl.pallas_call(
        layer,
        out_shape=[shape((1, 1, edges), f32)] + [shape((3, 3 * atoms), f32)] * 3,
        in_specs=vmem(16),
        out_specs=vmem(4),
        name="layer",
        compiler_params=grant(8),
    )(slab, y_in, y_out, *prepared, w2_copy, we_copy)

    r_out = lax.ppermute(f_out, "gy", pair_out("gy"))
    r_in = lax.ppermute(f_in, "gy", pair_in("gy"))
    column = f_own + r_out + r_in
    s_out = lax.ppermute(column[:, 2 * atoms :], "gx", pair_out("gx"))
    s_in = lax.ppermute(column[:, atoms : 2 * atoms], "gx", pair_in("gx"))
    forces = column[:, :atoms] + s_out + s_in
    return (energy, forces[None, None])


def solution(mesh):
    return jax.shard_map(
        body,
        mesh=mesh,
        in_specs=(
            P("gx", "gy", None, None),
            P("gx", "gy", None, None),
            P(),
            P("gx", "gy", None),
            P("gx", "gy", None),
            P("gx", "gy", None),
            P(),
            P(),
            P(),
            P(),
            P(),
            P(),
        ),
        out_specs=(P("gx", "gy", None), P("gx", "gy", None, None)),
        check_vma=False,
    )
```

```python
import math

import jax
import jax.numpy as jnp
from jax import lax
from jax.experimental import pallas as pl
from jax.experimental.pallas import tpu as pltpu
from jax.sharding import PartitionSpec as P

NBASIS = 8
EBLK = 64
POS_ROWS = 16

ROOT_THREE = math.sqrt(3.0)
ROOT_FIFTEEN = math.sqrt(15.0)
ROOT_FIVE = math.sqrt(5.0)
GAMMAS = [0.25 * 1.5**k for k in range(NBASIS)]

NN = (((1,), (0,)), ((), ()))
NT = (((1,), (1,)), ((), ()))


def mm(a, b, dims=NN):
    return lax.dot_general(a, b, dims, preferred_element_type=jnp.float32)


def turned(w):
    return w.astype(jnp.float32).T


def halves(x):
    high = x.astype(jnp.bfloat16).astype(jnp.float32)
    return high, x - high


def prepare(
    feats_hbm,
    positions_hbm,
    count_hbm,
    center_hbm,
    neighbor_hbm,
    valid_hbm,
    w_center_hbm,
    w_neighbor_hbm,
    w_radial_hbm,
    w_second_hbm,
    w_env_hbm,
    readout_hbm,
    hot_nb,
    hot_c,
    same,
    near,
    aux,
    wn_t,
    w2_t,
    we_t,
    wr_t,
    wr16,
    read_b,
    w2_copy,
    we_copy,
    feats,
    positions,
    atom_count,
    center,
    neighbor,
    valid,
    w_center,
    w_neighbor,
    w_radial,
    readout,
    sems,
):
    moves = [
        pltpu.make_async_copy(source, target, sems.at[k])
        for k, (source, target) in enumerate(
            (
                (neighbor_hbm, neighbor),
                (center_hbm, center),
                (valid_hbm, valid),
                (count_hbm, atom_count),
                (feats_hbm, feats),
                (positions_hbm, positions),
                (w_center_hbm, w_center),
                (w_neighbor_hbm, w_neighbor),
                (w_second_hbm, w2_copy),
                (w_env_hbm, we_copy),
                (w_radial_hbm, w_radial),
                (readout_hbm, readout),
            )
        )
    ]
    for move in moves:
        move.start()
    atoms = feats.shape[2]
    edges = center.shape[2]
    gx, gy = lax.axis_index("gx"), lax.axis_index("gy")
    for move in moves[:4]:
        move.wait()
    c_row = center[0]
    n_row = neighbor[0]
    slot = n_row // atoms
    atom = n_row - slot * atoms
    row_a = jnp.where(slot >= 3, 1, 0) + jnp.where(slot >= 6, 1, 0)
    row_b = slot - 3 * row_a
    in_a = 2 - 2 * (gx % 2)
    in_b = 2 - 2 * (gy % 2)
    place_x = jnp.where(row_a == 1, 0, jnp.where(row_a == in_a, 1, 2))
    place_y = jnp.where(row_b == 1, 0, jnp.where(row_b == in_b, 1, 2))
    local = (3 * place_y + place_x) * atoms + atom
    stacked = jnp.concatenate(
        [
            jnp.broadcast_to(local.astype(jnp.float32), (8, edges)),
            jnp.broadcast_to(c_row.astype(jnp.float32), (8, edges)),
        ],
        axis=0,
    ).T
    n_col = stacked[:, 0:1].astype(jnp.int32)
    c_col = stacked[:, 8:9].astype(jnp.int32)
    lane = lax.broadcasted_iota(jnp.int32, (edges, atoms), 1)
    for part in range(9):
        hot_nb[:, part * atoms : (part + 1) * atoms] = jnp.where(
            lane == n_col - part * atoms, 1.0, 0.0
        ).astype(jnp.bfloat16)
    c_hot = jnp.where(lane == c_col, 1.0, 0.0).astype(jnp.bfloat16)
    hot_c[...] = c_hot
    same[...] = jnp.where(c_col == c_row, 1.0, 0.0).astype(jnp.bfloat16)

    for move in moves[4:]:
        move.wait()
    near_all = mm(feats[0, 0], w_center[...]).astype(jnp.bfloat16)
    near[...] = mm(c_hot, near_all).T
    pos16 = jnp.concatenate(
        [positions[0, 0].astype(jnp.float32), jnp.zeros((13, atoms), jnp.float32)], axis=0
    ).astype(jnp.bfloat16)
    pos_c = mm(pos16, c_hot, NT)
    here = (lax.broadcasted_iota(jnp.int32, atom_count.shape, 0) == gx) & (
        lax.broadcasted_iota(jnp.int32, atom_count.shape, 1) == gy
    )
    count = jnp.where(here, atom_count[...], 0).astype(jnp.float32)
    count = jnp.sum(jnp.sum(count, axis=1, keepdims=True), axis=0, keepdims=True)
    used = (count.astype(jnp.int32) * (edges // EBLK) + atoms - 1) // atoms
    block = lax.broadcasted_iota(jnp.int32, (1, edges), 1) // EBLK
    mask = jnp.where(block < used, valid[0], 0).astype(jnp.float32)
    aux[...] = jnp.concatenate(
        [
            (row_a - 1).astype(jnp.float32),
            (row_b - 1).astype(jnp.float32),
            jnp.zeros((1, edges), jnp.float32),
            mask,
            jnp.zeros((4, edges), jnp.float32),
            pos_c[0:8],
        ],
        axis=0,
    )

    wn_t[...] = turned(w_neighbor[...]).astype(jnp.bfloat16)
    w2_t[...] = turned(w2_copy[...]).astype(jnp.bfloat16)
    we_t[...] = turned(we_copy[...]).astype(jnp.bfloat16)
    high, low = halves(w_radial[...])
    wr16[...] = jnp.concatenate([high, low], axis=0).astype(jnp.bfloat16)
    wr_t[...] = (
        jnp.concatenate([high, high, low, jnp.zeros_like(high)], axis=0).T.astype(jnp.bfloat16)
    )
    channels = w_center.shape[0]
    read_t = jnp.concatenate(
        [readout[...], jnp.zeros((5, channels), jnp.float32)], axis=0
    ).T
    for level in range(3):
        read_b[level] = jnp.broadcast_to(read_t[:, level : level + 1], (channels, edges))


def layer(
    slab_own,
    slab_in,
    slab_out,
    hot_nb,
    hot_c,
    same,
    near,
    aux,
    wn_t,
    w2_t,
    we_t,
    wr_t,
    wr16,
    read_b,
    w_second,
    w_env,
    energy,
    f_own,
    f_up,
    f_down,
):
    bf16, f32 = jnp.bfloat16, jnp.float32
    channels, edges = near.shape
    atoms = hot_c.shape[1]
    wide = 3 * atoms
    rows_nb = jnp.zeros((edges, channels), f32)
    pos_nb = jnp.zeros((8, edges), f32)
    for part, slab in enumerate((slab_own, slab_in, slab_out)):
        hot = hot_nb[:, part * wide : (part + 1) * wide]
        rows_nb = rows_nb + mm(hot, slab[0:wide])
        packed = slab[wide : wide + 3 * POS_ROWS].astype(f32)
        pos = jnp.concatenate([packed[8 * k : 8 * k + 8] for k in range(6)], axis=1)
        pos = jnp.concatenate([pos, jnp.zeros_like(pos)], axis=0).astype(bf16)
        pos_nb = pos_nb + mm(pos, hot, NT)[0:8]
    far = mm(wn_t[...], rows_nb.astype(bf16), NT).astype(bf16).astype(f32)

    mask = aux[3:4]
    d = pos_nb[0:3] + aux[0:3] - aux[8:11]
    dist_sq = jnp.sum(d * d, axis=0, keepdims=True) + 0.25
    inv = lax.rsqrt(dist_sq)
    dist = jnp.sqrt(dist_sq)
    u = d / dist
    ux, uy, uz = u[0:1], u[1:2], u[2:3]
    sub = lax.broadcasted_iota(jnp.int32, (NBASIS, edges), 0)
    gamma = jnp.full((NBASIS, edges), GAMMAS[0], f32)
    for k in range(1, NBASIS):
        gamma = jnp.where(sub == k, GAMMAS[k], gamma)
    basis = jnp.exp(-gamma * dist_sq)
    b_high, b_low = halves(basis)
    b32 = jnp.concatenate([b_high, b_low, b_high, jnp.zeros_like(b_high)], axis=0).astype(bf16)
    radial = mm(wr_t[...], b32)
    pre = (near[...] + far + radial).astype(bf16).astype(f32)
    sig = jax.nn.sigmoid(pre)
    latent = jnp.tanh(mm(w2_t[...], (pre * sig).astype(bf16))).astype(bf16)
    env = mm(we_t[...], latent) * mask
    harm = [
        None,
        ROOT_THREE * ux,
        ROOT_THREE * uy,
        ROOT_THREE * uz,
        ROOT_FIFTEEN * ux * uy,
        ROOT_FIFTEEN * uy * uz,
        0.5 * ROOT_FIVE * (3.0 * uz * uz - 1.0),
        ROOT_FIFTEEN * ux * uz,
        0.5 * ROOT_FIFTEEN * (ux * ux - uy * uy),
    ]
    term = jnp.sum(read_b[0] * env[0:channels], axis=0, keepdims=True)
    grads = [read_b[0] * mask]
    hg = [None] * 9
    for level, comps in ((1, (1, 2, 3)), (2, (4, 5, 6, 7, 8))):
        part = env[level * channels : (level + 1) * channels]
        twice = 2.0 * read_b[level]
        scaled = twice * part
        total = jnp.zeros((channels, edges), f32)
        for m in comps:
            gathered = mm((part * harm[m]).astype(bf16), same[...])
            hg[m] = jnp.sum(gathered * scaled, axis=0, keepdims=True)
            total = total + gathered * harm[m]
            term = term + 0.5 * harm[m] * hg[m]
        grads.append(twice * total * mask)
    env_grad = jnp.concatenate(grads, axis=0).astype(bf16)
    lat = latent.astype(f32)
    act_grad = (mm(w_env[...], env_grad) * (1.0 - lat * lat)).astype(bf16)
    pre_grad = mm(w_second[...], act_grad) * sig * (1.0 + pre * (1.0 - sig))
    p_high, p_low = halves(pre_grad)
    both = mm(wr16[...], p_high.astype(bf16)) + mm(wr16[...], p_low.astype(bf16))
    basis_grad = both[0:NBASIS] + both[NBASIS : 2 * NBASIS]
    ds = -jnp.sum(gamma * basis * basis_grad, axis=0, keepdims=True)
    gx = ROOT_THREE * hg[1] + ROOT_FIFTEEN * (uy * hg[4] + uz * hg[7] + ux * hg[8])
    gy = ROOT_THREE * hg[2] + ROOT_FIFTEEN * (ux * hg[4] + uz * hg[5] - uy * hg[8])
    gz = ROOT_THREE * hg[3] + ROOT_FIFTEEN * (uy * hg[5] + ux * hg[7]) + 3.0 * ROOT_FIVE * uz * hg[6]
    ds = ds - 0.5 * inv * inv * (gx * ux + gy * uy + gz * uz)
    g = jnp.concatenate([gx, gy, gz], axis=0)
    dg = g * inv + 2.0 * d * ds
    four_high, four_low = halves(jnp.concatenate([dg, term], axis=0))
    lines = jnp.concatenate([four_high, four_low, jnp.zeros((8, edges), f32)], axis=0).astype(bf16)
    to_c = mm(lines, hot_c[...])
    to_c = to_c[0:4] + to_c[4:8]
    energy[0] = to_c[3:4]
    parts = []
    for part in range(3):
        to_nb = mm(lines, hot_nb[:, part * wide : (part + 1) * wide])
        parts.append(-(to_nb[0:3] + to_nb[4:7]))
    f_own[:, 0:atoms] = parts[0][:, 0:atoms] + to_c[0:3]
    f_own[:, atoms:wide] = parts[0][:, atoms:wide]
    upper_in = lax.axis_index("gy") % 2 == 0
    f_up[...] = jnp.where(upper_in, parts[1], parts[2])
    f_down[...] = jnp.where(upper_in, parts[2], parts[1])


def pack(feats, positions, packed, pos, sems):
    atoms = feats.shape[2]
    half = atoms // 2
    move_pos = pltpu.make_async_copy(positions.at[0, 0], pos, sems.at[0])
    move_feats = pltpu.make_async_copy(feats.at[0, 0], packed.at[0:atoms], sems.at[1])
    move_pos.start()
    move_feats.start()
    move_pos.wait()
    rows = pos[...].astype(jnp.float32)
    gap = jnp.zeros((5, half), jnp.float32)
    packed[atoms : atoms + POS_ROWS] = jnp.concatenate(
        [rows[:, :half], gap, rows[:, half:], gap], axis=0
    ).astype(jnp.bfloat16)
    move_feats.wait()


def assemble(own, x_in, x_out, slab):
    atoms = own.shape[0] - POS_ROWS
    for k, part in enumerate((own, x_in, x_out)):
        slab[k * atoms : (k + 1) * atoms] = part[0:atoms]
        start = 3 * atoms + k * POS_ROWS
        slab[start : start + POS_ROWS] = part[atoms : atoms + POS_ROWS]


def grant(mib):
    return pltpu.CompilerParams(vmem_limit_bytes=mib << 20)


def vmem(n):
    return [pl.BlockSpec(memory_space=pltpu.VMEM)] * n


def in_hbm(*arrays):
    return [pltpu.with_memory_space_constraint(a, pltpu.HBM) for a in arrays]


def hbm(n):
    return [pl.BlockSpec(memory_space=pltpu.HBM)] * n


def pair_in(axis):
    return [(i, i ^ 1) for i in range(lax.axis_size(axis))]


def pair_out(axis):
    count = lax.axis_size(axis)
    return [(i, (i + 1) % count if i % 2 else (i - 1) % count) for i in range(count)]


def step_by(axis, distance):
    count = lax.axis_size(axis)
    return [(i, (i + distance) % count) for i in range(count)]


def body(
    feats,
    positions,
    atom_count,
    edge_center,
    edge_neighbor,
    edge_valid,
    w_center,
    w_neighbor,
    w_radial,
    w_second,
    w_env,
    readout,
):
    f32, bf16 = jnp.float32, jnp.bfloat16
    atoms, channels = feats.shape[2:]
    edges = edge_center.shape[2]
    shape = jax.ShapeDtypeStruct
    own = pl.pallas_call(
        pack,
        out_shape=shape((atoms + POS_ROWS, channels), bf16),
        in_specs=hbm(2),
        out_specs=pl.BlockSpec(memory_space=pltpu.VMEM),
        scratch_shapes=[pltpu.VMEM((3, atoms), bf16), pltpu.SemaphoreType.DMA((2,))],
        name="pack",
        compiler_params=grant(2),
    )(*in_hbm(feats, positions))
    x_out = lax.ppermute(own, "gx", pair_out("gx"))
    x_in = lax.ppermute(own, "gx", pair_in("gx"))

    *prepared, w2_copy, we_copy = pl.pallas_call(
        prepare,
        out_shape=[
            shape((edges, 9 * atoms), bf16),
            shape((edges, atoms), bf16),
            shape((edges, edges), bf16),
            shape((channels, edges), f32),
            shape((16, edges), f32),
            shape((channels, channels), bf16),
            shape((channels, channels), bf16),
            shape((3 * channels, channels), bf16),
            shape((channels, 4 * NBASIS), bf16),
            shape((2 * NBASIS, channels), bf16),
            shape((3, channels, edges), f32),
            shape((channels, channels), bf16),
            shape((channels, 3 * channels), bf16),
        ],
        in_specs=hbm(12),
        out_specs=vmem(13),
        scratch_shapes=[
            pltpu.VMEM(part.shape, part.dtype)
            for part in (
                feats,
                positions,
                atom_count,
                edge_center,
                edge_neighbor,
                edge_valid,
                w_center,
                w_neighbor,
                w_radial,
                readout,
            )
        ]
        + [pltpu.SemaphoreType.DMA((12,))],
        name="prepare",
        compiler_params=grant(8),
        cost_estimate=pl.CostEstimate(flops=100000000, bytes_accessed=3000000, transcendentals=0),
    )(
        *in_hbm(
            feats,
            positions,
            atom_count,
            edge_center,
            edge_neighbor,
            edge_valid,
            w_center,
            w_neighbor,
            w_radial,
            w_second,
            w_env,
            readout,
        )
    )

    slab = pl.pallas_call(
        assemble,
        out_shape=shape((3 * (atoms + POS_ROWS), channels), bf16),
        in_specs=vmem(3),
        out_specs=pl.BlockSpec(memory_space=pltpu.VMEM),
        name="assemble",
        compiler_params=grant(2),
    )(own, x_in, x_out)
    y_out = lax.ppermute(slab, "gy", pair_out("gy"))
    y_in = lax.ppermute(slab, "gy", pair_in("gy"))

    energy, f_own, f_up, f_down = pl.pallas_call(
        layer,
        out_shape=[shape((1, 1, edges), f32)] + [shape((3, 3 * atoms), f32)] * 3,
        in_specs=vmem(16),
        out_specs=vmem(4),
        name="layer",
        compiler_params=grant(8),
    )(slab, y_in, y_out, *prepared, w2_copy, we_copy)

    r_up = lax.ppermute(f_up, "gy", step_by("gy", 1))
    r_down = lax.ppermute(f_down, "gy", step_by("gy", -1))
    column = f_own + r_up + r_down
    s_out = lax.ppermute(column[:, 2 * atoms :], "gx", pair_out("gx"))
    s_in = lax.ppermute(column[:, atoms : 2 * atoms], "gx", pair_in("gx"))
    forces = column[:, :atoms] + s_out + s_in
    return (energy, forces[None, None])


def solution(mesh):
    return jax.shard_map(
        body,
        mesh=mesh,
        in_specs=(
            P("gx", "gy", None, None),
            P("gx", "gy", None, None),
            P(),
            P("gx", "gy", None),
            P("gx", "gy", None),
            P("gx", "gy", None),
            P(),
            P(),
            P(),
            P(),
            P(),
            P(),
        ),
        out_specs=(P("gx", "gy", None), P("gx", "gy", None, None)),
        check_vma=False,
    )
```

```python
import math

import jax
import jax.numpy as jnp
from jax import lax
from jax.experimental import pallas as pl
from jax.experimental.pallas import tpu as pltpu
from jax.sharding import PartitionSpec as P

NBASIS = 8
EBLK = 64
POS_ROWS = 16

ROOT_THREE = math.sqrt(3.0)
ROOT_FIFTEEN = math.sqrt(15.0)
ROOT_FIVE = math.sqrt(5.0)
GAMMAS = [0.25 * 1.5**k for k in range(NBASIS)]

NN = (((1,), (0,)), ((), ()))
NT = (((1,), (1,)), ((), ()))


def mm(a, b, dims=NN):
    return lax.dot_general(a, b, dims, preferred_element_type=jnp.float32)


def turned(w):
    return w.astype(jnp.float32).T


def halves(x):
    high = x.astype(jnp.bfloat16).astype(jnp.float32)
    return high, x - high


def prepare(
    slab,
    feats_hbm,
    positions_hbm,
    count_hbm,
    center_hbm,
    neighbor_hbm,
    valid_hbm,
    w_center_hbm,
    w_neighbor_hbm,
    w_radial_hbm,
    w_second_hbm,
    w_env_hbm,
    readout_hbm,
    hot_nb,
    hot_c,
    same,
    near,
    aux,
    wn_t,
    w2_t,
    we_t,
    wr_t,
    wr16,
    read_b,
    w2_copy,
    we_copy,
    rows_own,
    pos_own,
    feats,
    positions,
    atom_count,
    center,
    neighbor,
    valid,
    w_center,
    w_neighbor,
    w_radial,
    readout,
    sems,
):
    moves = [
        pltpu.make_async_copy(source, target, sems.at[k])
        for k, (source, target) in enumerate(
            (
                (neighbor_hbm, neighbor),
                (center_hbm, center),
                (valid_hbm, valid),
                (count_hbm, atom_count),
                (feats_hbm, feats),
                (positions_hbm, positions),
                (w_center_hbm, w_center),
                (w_neighbor_hbm, w_neighbor),
                (w_second_hbm, w2_copy),
                (w_env_hbm, we_copy),
                (w_radial_hbm, w_radial),
                (readout_hbm, readout),
            )
        )
    ]
    for move in moves:
        move.start()
    atoms = feats.shape[2]
    edges = center.shape[2]
    gx, gy = lax.axis_index("gx"), lax.axis_index("gy")
    for move in moves[:4]:
        move.wait()
    c_row = center[0]
    n_row = neighbor[0]
    slot = n_row // atoms
    atom = n_row - slot * atoms
    row_a = jnp.where(slot >= 3, 1, 0) + jnp.where(slot >= 6, 1, 0)
    row_b = slot - 3 * row_a
    in_a = 2 - 2 * (gx % 2)
    in_b = 2 - 2 * (gy % 2)
    place_x = jnp.where(row_a == 1, 0, jnp.where(row_a == in_a, 1, 2))
    place_y = jnp.where(row_b == 1, 0, jnp.where(row_b == in_b, 1, 2))
    local = (3 * place_y + place_x) * atoms + atom
    stacked = jnp.concatenate(
        [
            jnp.broadcast_to(local.astype(jnp.float32), (8, edges)),
            jnp.broadcast_to(c_row.astype(jnp.float32), (8, edges)),
        ],
        axis=0,
    ).T
    n_col = stacked[:, 0:1].astype(jnp.int32)
    c_col = stacked[:, 8:9].astype(jnp.int32)
    lane = lax.broadcasted_iota(jnp.int32, (edges, atoms), 1)
    for part in range(9):
        hot_nb[:, part * atoms : (part + 1) * atoms] = jnp.where(
            lane == n_col - part * atoms, 1.0, 0.0
        ).astype(jnp.bfloat16)
    wide = 3 * atoms
    hot = hot_nb[:, 0:wide]
    rows_own[...] = mm(hot, slab[0:wide])
    packed = slab[wide : wide + 3 * POS_ROWS].astype(jnp.float32)
    pos = jnp.concatenate([packed[8 * k : 8 * k + 8] for k in range(6)], axis=1)
    pos = jnp.concatenate([pos, jnp.zeros_like(pos)], axis=0).astype(jnp.bfloat16)
    pos_own[...] = mm(pos, hot, NT)[0:8]
    c_hot = jnp.where(lane == c_col, 1.0, 0.0).astype(jnp.bfloat16)
    hot_c[...] = c_hot
    same[...] = jnp.where(c_col == c_row, 1.0, 0.0).astype(jnp.bfloat16)

    for move in moves[4:]:
        move.wait()
    near_all = mm(feats[0, 0], w_center[...]).astype(jnp.bfloat16)
    near[...] = mm(c_hot, near_all).T
    pos16 = jnp.concatenate(
        [positions[0, 0].astype(jnp.float32), jnp.zeros((13, atoms), jnp.float32)], axis=0
    ).astype(jnp.bfloat16)
    pos_c = mm(pos16, c_hot, NT)
    here = (lax.broadcasted_iota(jnp.int32, atom_count.shape, 0) == gx) & (
        lax.broadcasted_iota(jnp.int32, atom_count.shape, 1) == gy
    )
    count = jnp.where(here, atom_count[...], 0).astype(jnp.float32)
    count = jnp.sum(jnp.sum(count, axis=1, keepdims=True), axis=0, keepdims=True)
    used = (count.astype(jnp.int32) * (edges // EBLK) + atoms - 1) // atoms
    block = lax.broadcasted_iota(jnp.int32, (1, edges), 1) // EBLK
    mask = jnp.where(block < used, valid[0], 0).astype(jnp.float32)
    aux[...] = jnp.concatenate(
        [
            (row_a - 1).astype(jnp.float32),
            (row_b - 1).astype(jnp.float32),
            jnp.zeros((1, edges), jnp.float32),
            mask,
            jnp.zeros((4, edges), jnp.float32),
            pos_c[0:8],
        ],
        axis=0,
    )

    wn_t[...] = turned(w_neighbor[...]).astype(jnp.bfloat16)
    w2_t[...] = turned(w2_copy[...]).astype(jnp.bfloat16)
    we_t[...] = turned(we_copy[...]).astype(jnp.bfloat16)
    high, low = halves(w_radial[...])
    wr16[...] = jnp.concatenate([high, low], axis=0).astype(jnp.bfloat16)
    wr_t[...] = (
        jnp.concatenate([high, high, low, jnp.zeros_like(high)], axis=0).T.astype(jnp.bfloat16)
    )
    channels = w_center.shape[0]
    read_t = jnp.concatenate(
        [readout[...], jnp.zeros((5, channels), jnp.float32)], axis=0
    ).T
    for level in range(3):
        read_b[level] = jnp.broadcast_to(read_t[:, level : level + 1], (channels, edges))


def layer(
    slab_in,
    slab_out,
    hot_nb,
    hot_c,
    same,
    near,
    aux,
    wn_t,
    w2_t,
    we_t,
    wr_t,
    wr16,
    read_b,
    w_second,
    w_env,
    rows_own,
    pos_own,
    energy,
    f_own,
    f_in,
    f_out,
):
    bf16, f32 = jnp.bfloat16, jnp.float32
    channels, edges = near.shape
    atoms = hot_c.shape[1]
    wide = 3 * atoms
    rows_nb = rows_own[...]
    pos_nb = pos_own[...]
    for part, slab in enumerate((slab_in, slab_out), 1):
        hot = hot_nb[:, part * wide : (part + 1) * wide]
        rows_nb = rows_nb + mm(hot, slab[0:wide])
        packed = slab[wide : wide + 3 * POS_ROWS].astype(f32)
        pos = jnp.concatenate([packed[8 * k : 8 * k + 8] for k in range(6)], axis=1)
        pos = jnp.concatenate([pos, jnp.zeros_like(pos)], axis=0).astype(bf16)
        pos_nb = pos_nb + mm(pos, hot, NT)[0:8]
    far = mm(wn_t[...], rows_nb.astype(bf16), NT).astype(bf16).astype(f32)

    mask = aux[3:4]
    d = pos_nb[0:3] + aux[0:3] - aux[8:11]
    dist_sq = jnp.sum(d * d, axis=0, keepdims=True) + 0.25
    inv = lax.rsqrt(dist_sq)
    dist = jnp.sqrt(dist_sq)
    u = d / dist
    ux, uy, uz = u[0:1], u[1:2], u[2:3]
    sub = lax.broadcasted_iota(jnp.int32, (NBASIS, edges), 0)
    gamma = jnp.full((NBASIS, edges), GAMMAS[0], f32)
    for k in range(1, NBASIS):
        gamma = jnp.where(sub == k, GAMMAS[k], gamma)
    basis = jnp.exp(-gamma * dist_sq)
    b_high, b_low = halves(basis)
    b32 = jnp.concatenate([b_high, b_low, b_high, jnp.zeros_like(b_high)], axis=0).astype(bf16)
    radial = mm(wr_t[...], b32)
    pre = (near[...] + far + radial).astype(bf16).astype(f32)
    sig = jax.nn.sigmoid(pre)
    latent = jnp.tanh(mm(w2_t[...], (pre * sig).astype(bf16))).astype(bf16)
    env = mm(we_t[...], latent) * mask
    harm = [
        None,
        ROOT_THREE * ux,
        ROOT_THREE * uy,
        ROOT_THREE * uz,
        ROOT_FIFTEEN * ux * uy,
        ROOT_FIFTEEN * uy * uz,
        0.5 * ROOT_FIVE * (3.0 * uz * uz - 1.0),
        ROOT_FIFTEEN * ux * uz,
        0.5 * ROOT_FIFTEEN * (ux * ux - uy * uy),
    ]
    term = jnp.sum(read_b[0] * env[0:channels], axis=0, keepdims=True)
    grads = [read_b[0] * mask]
    hg = [None] * 9
    for level, comps in ((1, (1, 2, 3)), (2, (4, 5, 6, 7, 8))):
        part = env[level * channels : (level + 1) * channels]
        twice = 2.0 * read_b[level]
        scaled = twice * part
        total = jnp.zeros((channels, edges), f32)
        for m in comps:
            gathered = mm((part * harm[m]).astype(bf16), same[...])
            hg[m] = jnp.sum(gathered * scaled, axis=0, keepdims=True)
            total = total + gathered * harm[m]
            term = term + 0.5 * harm[m] * hg[m]
        grads.append(twice * total * mask)
    env_grad = jnp.concatenate(grads, axis=0).astype(bf16)
    lat = latent.astype(f32)
    act_grad = (mm(w_env[...], env_grad) * (1.0 - lat * lat)).astype(bf16)
    pre_grad = mm(w_second[...], act_grad) * sig * (1.0 + pre * (1.0 - sig))
    p_high, p_low = halves(pre_grad)
    both = mm(wr16[...], p_high.astype(bf16)) + mm(wr16[...], p_low.astype(bf16))
    basis_grad = both[0:NBASIS] + both[NBASIS : 2 * NBASIS]
    ds = -jnp.sum(gamma * basis * basis_grad, axis=0, keepdims=True)
    gx = ROOT_THREE * hg[1] + ROOT_FIFTEEN * (uy * hg[4] + uz * hg[7] + ux * hg[8])
    gy = ROOT_THREE * hg[2] + ROOT_FIFTEEN * (ux * hg[4] + uz * hg[5] - uy * hg[8])
    gz = ROOT_THREE * hg[3] + ROOT_FIFTEEN * (uy * hg[5] + ux * hg[7]) + 3.0 * ROOT_FIVE * uz * hg[6]
    ds = ds - 0.5 * inv * inv * (gx * ux + gy * uy + gz * uz)
    g = jnp.concatenate([gx, gy, gz], axis=0)
    dg = g * inv + 2.0 * d * ds
    four_high, four_low = halves(jnp.concatenate([dg, term], axis=0))
    lines = jnp.concatenate([four_high, four_low, jnp.zeros((8, edges), f32)], axis=0).astype(bf16)
    to_c = mm(lines, hot_c[...])
    to_c = to_c[0:4] + to_c[4:8]
    energy[0] = to_c[3:4]
    upper_in = lax.axis_index("gx") % 2 == 0
    for part, out in enumerate((f_own, f_in, f_out)):
        to_nb = mm(lines, hot_nb[:, part * wide : (part + 1) * wide])
        to_nb = -(to_nb[0:3] + to_nb[4:7])
        mine, inner, outer = (to_nb[:, k * atoms : (k + 1) * atoms] for k in range(3))
        out[:, 0:atoms] = mine + to_c[0:3] if part == 0 else mine
        out[:, atoms : 2 * atoms] = jnp.where(upper_in, inner, outer)
        out[:, 2 * atoms : wide] = jnp.where(upper_in, outer, inner)


def pack(feats, positions, packed, pos, sems):
    atoms = feats.shape[2]
    half = atoms // 2
    move_pos = pltpu.make_async_copy(positions.at[0, 0], pos, sems.at[0])
    move_feats = pltpu.make_async_copy(feats.at[0, 0], packed.at[0:atoms], sems.at[1])
    move_pos.start()
    move_feats.start()
    move_pos.wait()
    rows = pos[...].astype(jnp.float32)
    gap = jnp.zeros((5, half), jnp.float32)
    packed[atoms : atoms + POS_ROWS] = jnp.concatenate(
        [rows[:, :half], gap, rows[:, half:], gap], axis=0
    ).astype(jnp.bfloat16)
    move_feats.wait()


def assemble(own, x_in, x_out, slab):
    atoms = own.shape[0] - POS_ROWS
    for k, part in enumerate((own, x_in, x_out)):
        slab[k * atoms : (k + 1) * atoms] = part[0:atoms]
        start = 3 * atoms + k * POS_ROWS
        slab[start : start + POS_ROWS] = part[atoms : atoms + POS_ROWS]


def grant(mib):
    return pltpu.CompilerParams(vmem_limit_bytes=mib << 20)


def vmem(n):
    return [pl.BlockSpec(memory_space=pltpu.VMEM)] * n


def in_hbm(*arrays):
    return [pltpu.with_memory_space_constraint(a, pltpu.HBM) for a in arrays]


def hbm(n):
    return [pl.BlockSpec(memory_space=pltpu.HBM)] * n


def pair_in(axis):
    return [(i, i ^ 1) for i in range(lax.axis_size(axis))]


def pair_out(axis):
    count = lax.axis_size(axis)
    return [(i, (i + 1) % count if i % 2 else (i - 1) % count) for i in range(count)]


def step_by(axis, distance):
    count = lax.axis_size(axis)
    return [(i, (i + distance) % count) for i in range(count)]


def body(
    feats,
    positions,
    atom_count,
    edge_center,
    edge_neighbor,
    edge_valid,
    w_center,
    w_neighbor,
    w_radial,
    w_second,
    w_env,
    readout,
):
    f32, bf16 = jnp.float32, jnp.bfloat16
    atoms, channels = feats.shape[2:]
    edges = edge_center.shape[2]
    shape = jax.ShapeDtypeStruct
    own = pl.pallas_call(
        pack,
        out_shape=shape((atoms + POS_ROWS, channels), bf16),
        in_specs=hbm(2),
        out_specs=pl.BlockSpec(memory_space=pltpu.VMEM),
        scratch_shapes=[pltpu.VMEM((3, atoms), bf16), pltpu.SemaphoreType.DMA((2,))],
        name="pack",
        compiler_params=grant(2),
    )(*in_hbm(feats, positions))
    x_out = lax.ppermute(own, "gx", pair_out("gx"))
    x_in = lax.ppermute(own, "gx", pair_in("gx"))

    slab = pl.pallas_call(
        assemble,
        out_shape=shape((3 * (atoms + POS_ROWS), channels), bf16),
        in_specs=vmem(3),
        out_specs=pl.BlockSpec(memory_space=pltpu.VMEM),
        name="assemble",
        compiler_params=grant(2),
    )(own, x_in, x_out)
    y_out = lax.ppermute(slab, "gy", pair_out("gy"))
    y_in = lax.ppermute(slab, "gy", pair_in("gy"))

    *prepared, w2_copy, we_copy, rows_own, pos_own = pl.pallas_call(
        prepare,
        out_shape=[
            shape((edges, 9 * atoms), bf16),
            shape((edges, atoms), bf16),
            shape((edges, edges), bf16),
            shape((channels, edges), f32),
            shape((16, edges), f32),
            shape((channels, channels), bf16),
            shape((channels, channels), bf16),
            shape((3 * channels, channels), bf16),
            shape((channels, 4 * NBASIS), bf16),
            shape((2 * NBASIS, channels), bf16),
            shape((3, channels, edges), f32),
            shape((channels, channels), bf16),
            shape((channels, 3 * channels), bf16),
            shape((edges, channels), f32),
            shape((8, edges), f32),
        ],
        in_specs=vmem(1) + hbm(12),
        out_specs=vmem(15),
        scratch_shapes=[
            pltpu.VMEM(part.shape, part.dtype)
            for part in (
                feats,
                positions,
                atom_count,
                edge_center,
                edge_neighbor,
                edge_valid,
                w_center,
                w_neighbor,
                w_radial,
                readout,
            )
        ]
        + [pltpu.SemaphoreType.DMA((12,))],
        name="prepare",
        compiler_params=grant(8),
        cost_estimate=pl.CostEstimate(flops=100000000, bytes_accessed=3000000, transcendentals=0),
    )(
        slab,
        *in_hbm(
            feats,
            positions,
            atom_count,
            edge_center,
            edge_neighbor,
            edge_valid,
            w_center,
            w_neighbor,
            w_radial,
            w_second,
            w_env,
            readout,
        )
    )

    energy, f_own, f_in, f_out = pl.pallas_call(
        layer,
        out_shape=[shape((1, 1, edges), f32)] + [shape((3, 3 * atoms), f32)] * 3,
        in_specs=vmem(17),
        out_specs=vmem(4),
        name="layer",
        compiler_params=grant(8),
    )(y_in, y_out, *prepared, w2_copy, we_copy, rows_own, pos_own)

    r_out = lax.ppermute(f_out, "gy", pair_out("gy"))
    r_in = lax.ppermute(f_in, "gy", pair_in("gy"))
    column = f_own + r_out + r_in
    s_up = lax.ppermute(column[:, atoms : 2 * atoms], "gx", step_by("gx", 1))
    s_down = lax.ppermute(column[:, 2 * atoms :], "gx", step_by("gx", -1))
    forces = column[:, :atoms] + s_up + s_down
    return (energy, forces[None, None])


def solution(mesh):
    return jax.shard_map(
        body,
        mesh=mesh,
        in_specs=(
            P("gx", "gy", None, None),
            P("gx", "gy", None, None),
            P(),
            P("gx", "gy", None),
            P("gx", "gy", None),
            P("gx", "gy", None),
            P(),
            P(),
            P(),
            P(),
            P(),
            P(),
        ),
        out_specs=(P("gx", "gy", None), P("gx", "gy", None, None)),
        check_vma=False,
    )
```

```python
import math

import jax
import jax.numpy as jnp
from jax import lax
from jax.experimental import pallas as pl
from jax.experimental.pallas import tpu as pltpu
from jax.sharding import PartitionSpec as P

NBASIS = 8
EBLK = 64
POS_ROWS = 16

ROOT_THREE = math.sqrt(3.0)
ROOT_FIFTEEN = math.sqrt(15.0)
ROOT_FIVE = math.sqrt(5.0)
GAMMAS = [0.25 * 1.5**k for k in range(NBASIS)]

NN = (((1,), (0,)), ((), ()))
NT = (((1,), (1,)), ((), ()))


def mm(a, b, dims=NN):
    return lax.dot_general(a, b, dims, preferred_element_type=jnp.float32)


def turned(w):
    return w.astype(jnp.float32).T


def halves(x):
    high = x.astype(jnp.bfloat16).astype(jnp.float32)
    return high, x - high


def prepare(
    slab,
    feats_hbm,
    positions_hbm,
    count_hbm,
    center_hbm,
    neighbor_hbm,
    valid_hbm,
    w_center_hbm,
    w_neighbor_hbm,
    w_radial_hbm,
    w_second_hbm,
    w_env_hbm,
    readout_hbm,
    hot_nb,
    hot_c,
    same,
    near,
    aux,
    wn_t,
    w2_t,
    we_t,
    wr_t,
    wr16,
    read_b,
    w2_copy,
    we_copy,
    rows_own,
    pos_own,
    feats,
    positions,
    atom_count,
    center,
    neighbor,
    valid,
    w_center,
    w_neighbor,
    w_radial,
    readout,
    sems,
):
    moves = [
        pltpu.make_async_copy(source, target, sems.at[k])
        for k, (source, target) in enumerate(
            (
                (neighbor_hbm, neighbor),
                (center_hbm, center),
                (valid_hbm, valid),
                (count_hbm, atom_count),
                (feats_hbm, feats),
                (positions_hbm, positions),
                (w_center_hbm, w_center),
                (w_neighbor_hbm, w_neighbor),
                (w_second_hbm, w2_copy),
                (w_env_hbm, we_copy),
                (w_radial_hbm, w_radial),
                (readout_hbm, readout),
            )
        )
    ]
    for move in moves:
        move.start()
    atoms = feats.shape[2]
    edges = center.shape[2]
    gx, gy = lax.axis_index("gx"), lax.axis_index("gy")
    for move in moves[:4]:
        move.wait()
    c_row = center[0]
    n_row = neighbor[0]
    slot = n_row // atoms
    atom = n_row - slot * atoms
    row_a = jnp.where(slot >= 3, 1, 0) + jnp.where(slot >= 6, 1, 0)
    row_b = slot - 3 * row_a
    in_a = 2 - 2 * (gx % 2)
    in_b = 2 - 2 * (gy % 2)
    place_x = jnp.where(row_a == 1, 0, jnp.where(row_a == in_a, 1, 2))
    place_y = jnp.where(row_b == 1, 0, jnp.where(row_b == in_b, 1, 2))
    local = (3 * place_y + place_x) * atoms + atom
    stacked = jnp.concatenate(
        [
            jnp.broadcast_to(local.astype(jnp.float32), (8, edges)),
            jnp.broadcast_to(c_row.astype(jnp.float32), (8, edges)),
        ],
        axis=0,
    ).T
    n_col = stacked[:, 0:1].astype(jnp.int32)
    c_col = stacked[:, 8:9].astype(jnp.int32)
    lane = lax.broadcasted_iota(jnp.int32, (edges, atoms), 1)
    for part in range(9):
        hot_nb[:, part * atoms : (part + 1) * atoms] = jnp.where(
            lane == n_col - part * atoms, 1.0, 0.0
        ).astype(jnp.bfloat16)
    wide = 3 * atoms
    hot = hot_nb[:, 0:wide]
    rows_own[...] = mm(hot, slab[0:wide])
    packed = slab[wide : wide + 3 * POS_ROWS].astype(jnp.float32)
    pos = jnp.concatenate([packed[8 * k : 8 * k + 8] for k in range(6)], axis=1)
    pos = jnp.concatenate([pos, jnp.zeros_like(pos)], axis=0).astype(jnp.bfloat16)
    pos_own[...] = mm(pos, hot, NT)[0:8]
    c_hot = jnp.where(lane == c_col, 1.0, 0.0).astype(jnp.bfloat16)
    hot_c[...] = c_hot
    same[...] = jnp.where(c_col == c_row, 1.0, 0.0).astype(jnp.bfloat16)

    for move in moves[4:]:
        move.wait()
    near_all = mm(feats[0, 0], w_center[...]).astype(jnp.bfloat16)
    near[...] = mm(c_hot, near_all).T
    pos16 = jnp.concatenate(
        [positions[0, 0].astype(jnp.float32), jnp.zeros((13, atoms), jnp.float32)], axis=0
    ).astype(jnp.bfloat16)
    pos_c = mm(pos16, c_hot, NT)
    here = (lax.broadcasted_iota(jnp.int32, atom_count.shape, 0) == gx) & (
        lax.broadcasted_iota(jnp.int32, atom_count.shape, 1) == gy
    )
    count = jnp.where(here, atom_count[...], 0).astype(jnp.float32)
    count = jnp.sum(jnp.sum(count, axis=1, keepdims=True), axis=0, keepdims=True)
    used = (count.astype(jnp.int32) * (edges // EBLK) + atoms - 1) // atoms
    block = lax.broadcasted_iota(jnp.int32, (1, edges), 1) // EBLK
    mask = jnp.where(block < used, valid[0], 0).astype(jnp.float32)
    aux[...] = jnp.concatenate(
        [
            (row_a - 1).astype(jnp.float32),
            (row_b - 1).astype(jnp.float32),
            jnp.zeros((1, edges), jnp.float32),
            mask,
            jnp.zeros((4, edges), jnp.float32),
            pos_c[0:8],
        ],
        axis=0,
    )

    wn_t[...] = turned(w_neighbor[...]).astype(jnp.bfloat16)
    w2_t[...] = turned(w2_copy[...]).astype(jnp.bfloat16)
    we_t[...] = turned(we_copy[...]).astype(jnp.bfloat16)
    high, low = halves(w_radial[...])
    wr16[...] = jnp.concatenate([high, low], axis=0).astype(jnp.bfloat16)
    wr_t[...] = (
        jnp.concatenate([high, high, low, jnp.zeros_like(high)], axis=0).T.astype(jnp.bfloat16)
    )
    channels = w_center.shape[0]
    read_t = jnp.concatenate(
        [readout[...], jnp.zeros((5, channels), jnp.float32)], axis=0
    ).T
    for level in range(3):
        read_b[level] = jnp.broadcast_to(read_t[:, level : level + 1], (channels, edges))


def layer(
    slab_in,
    slab_out,
    hot_nb,
    hot_c,
    same,
    near,
    aux,
    wn_t,
    w2_t,
    we_t,
    wr_t,
    wr16,
    read_b,
    w_second,
    w_env,
    rows_own,
    pos_own,
    f_own,
    f_in,
    f_out,
):
    bf16, f32 = jnp.bfloat16, jnp.float32
    channels, edges = near.shape
    atoms = hot_c.shape[1]
    wide = 3 * atoms
    rows_nb = rows_own[...]
    pos_nb = pos_own[...]
    for part, slab in enumerate((slab_in, slab_out), 1):
        hot = hot_nb[:, part * wide : (part + 1) * wide]
        rows_nb = rows_nb + mm(hot, slab[0:wide])
        packed = slab[wide : wide + 3 * POS_ROWS].astype(f32)
        pos = jnp.concatenate([packed[8 * k : 8 * k + 8] for k in range(6)], axis=1)
        pos = jnp.concatenate([pos, jnp.zeros_like(pos)], axis=0).astype(bf16)
        pos_nb = pos_nb + mm(pos, hot, NT)[0:8]
    far = mm(wn_t[...], rows_nb.astype(bf16), NT).astype(bf16).astype(f32)

    mask = aux[3:4]
    d = pos_nb[0:3] + aux[0:3] - aux[8:11]
    dist_sq = jnp.sum(d * d, axis=0, keepdims=True) + 0.25
    inv = lax.rsqrt(dist_sq)
    dist = jnp.sqrt(dist_sq)
    u = d / dist
    ux, uy, uz = u[0:1], u[1:2], u[2:3]
    sub = lax.broadcasted_iota(jnp.int32, (NBASIS, edges), 0)
    gamma = jnp.full((NBASIS, edges), GAMMAS[0], f32)
    for k in range(1, NBASIS):
        gamma = jnp.where(sub == k, GAMMAS[k], gamma)
    basis = jnp.exp(-gamma * dist_sq)
    b_high, b_low = halves(basis)
    b32 = jnp.concatenate([b_high, b_low, b_high, jnp.zeros_like(b_high)], axis=0).astype(bf16)
    radial = mm(wr_t[...], b32)
    pre = (near[...] + far + radial).astype(bf16).astype(f32)
    sig = jax.nn.sigmoid(pre)
    latent = jnp.tanh(mm(w2_t[...], (pre * sig).astype(bf16))).astype(bf16)
    env = mm(we_t[...], latent) * mask
    harm = [
        None,
        ROOT_THREE * ux,
        ROOT_THREE * uy,
        ROOT_THREE * uz,
        ROOT_FIFTEEN * ux * uy,
        ROOT_FIFTEEN * uy * uz,
        0.5 * ROOT_FIVE * (3.0 * uz * uz - 1.0),
        ROOT_FIFTEEN * ux * uz,
        0.5 * ROOT_FIFTEEN * (ux * ux - uy * uy),
    ]
    term = jnp.sum(read_b[0] * env[0:channels], axis=0, keepdims=True)
    grads = [read_b[0] * mask]
    hg = [None] * 9
    for level, comps in ((1, (1, 2, 3)), (2, (4, 5, 6, 7, 8))):
        part = env[level * channels : (level + 1) * channels]
        twice = 2.0 * read_b[level]
        scaled = twice * part
        total = jnp.zeros((channels, edges), f32)
        for m in comps:
            gathered = mm((part * harm[m]).astype(bf16), same[...])
            hg[m] = jnp.sum(gathered * scaled, axis=0, keepdims=True)
            total = total + gathered * harm[m]
            term = term + 0.5 * harm[m] * hg[m]
        grads.append(twice * total * mask)
    env_grad = jnp.concatenate(grads, axis=0).astype(bf16)
    lat = latent.astype(f32)
    act_grad = (mm(w_env[...], env_grad) * (1.0 - lat * lat)).astype(bf16)
    pre_grad = mm(w_second[...], act_grad) * sig * (1.0 + pre * (1.0 - sig))
    p_high, p_low = halves(pre_grad)
    both = mm(wr16[...], p_high.astype(bf16)) + mm(wr16[...], p_low.astype(bf16))
    basis_grad = both[0:NBASIS] + both[NBASIS : 2 * NBASIS]
    ds = -jnp.sum(gamma * basis * basis_grad, axis=0, keepdims=True)
    gx = ROOT_THREE * hg[1] + ROOT_FIFTEEN * (uy * hg[4] + uz * hg[7] + ux * hg[8])
    gy = ROOT_THREE * hg[2] + ROOT_FIFTEEN * (ux * hg[4] + uz * hg[5] - uy * hg[8])
    gz = ROOT_THREE * hg[3] + ROOT_FIFTEEN * (uy * hg[5] + ux * hg[7]) + 3.0 * ROOT_FIVE * uz * hg[6]
    ds = ds - 0.5 * inv * inv * (gx * ux + gy * uy + gz * uz)
    g = jnp.concatenate([gx, gy, gz], axis=0)
    dg = g * inv + 2.0 * d * ds
    four_high, four_low = halves(jnp.concatenate([dg, term], axis=0))
    lines = jnp.concatenate([four_high, four_low, jnp.zeros((8, edges), f32)], axis=0).astype(bf16)
    to_c = mm(lines, hot_c[...])
    to_c = to_c[0:4] + to_c[4:8]
    f_own[3:4, 0:atoms] = to_c[3:4]
    f_own[3:4, atoms:wide] = jnp.zeros((1, wide - atoms), f32)
    upper_in = lax.axis_index("gx") % 2 == 0
    for part, out in enumerate((f_own, f_in, f_out)):
        to_nb = mm(lines, hot_nb[:, part * wide : (part + 1) * wide])
        to_nb = -(to_nb[0:3] + to_nb[4:7])
        mine, inner, outer = (to_nb[:, k * atoms : (k + 1) * atoms] for k in range(3))
        out[0:3, 0:atoms] = mine + to_c[0:3] if part == 0 else mine
        out[0:3, atoms : 2 * atoms] = jnp.where(upper_in, inner, outer)
        out[0:3, 2 * atoms : wide] = jnp.where(upper_in, outer, inner)


def pack(feats, positions, packed, pos, sems):
    atoms = feats.shape[2]
    half = atoms // 2
    move_pos = pltpu.make_async_copy(positions.at[0, 0], pos, sems.at[0])
    move_feats = pltpu.make_async_copy(feats.at[0, 0], packed.at[0:atoms], sems.at[1])
    move_pos.start()
    move_feats.start()
    move_pos.wait()
    rows = pos[...].astype(jnp.float32)
    gap = jnp.zeros((5, half), jnp.float32)
    packed[atoms : atoms + POS_ROWS] = jnp.concatenate(
        [rows[:, :half], gap, rows[:, half:], gap], axis=0
    ).astype(jnp.bfloat16)
    move_feats.wait()


def assemble(own, x_out, x_in, slab):
    atoms = own.shape[0] - POS_ROWS
    for k, part in enumerate((own, x_in, x_out)):
        slab[k * atoms : (k + 1) * atoms] = part[0:atoms]
        start = 3 * atoms + k * POS_ROWS
        slab[start : start + POS_ROWS] = part[atoms : atoms + POS_ROWS]


def grant(mib):
    return pltpu.CompilerParams(vmem_limit_bytes=mib << 20)


def vmem(n):
    return [pl.BlockSpec(memory_space=pltpu.VMEM)] * n


def in_hbm(*arrays):
    return [pltpu.with_memory_space_constraint(a, pltpu.HBM) for a in arrays]


def hbm(n):
    return [pl.BlockSpec(memory_space=pltpu.HBM)] * n


def pair_in(axis):
    return [(i, i ^ 1) for i in range(lax.axis_size(axis))]


def pair_out(axis):
    count = lax.axis_size(axis)
    return [(i, (i + 1) % count if i % 2 else (i - 1) % count) for i in range(count)]


def step_by(axis, distance):
    count = lax.axis_size(axis)
    return [(i, (i + distance) % count) for i in range(count)]


def body(
    feats,
    positions,
    atom_count,
    edge_center,
    edge_neighbor,
    edge_valid,
    w_center,
    w_neighbor,
    w_radial,
    w_second,
    w_env,
    readout,
):
    f32, bf16 = jnp.float32, jnp.bfloat16
    atoms, channels = feats.shape[2:]
    edges = edge_center.shape[2]
    shape = jax.ShapeDtypeStruct
    own = pl.pallas_call(
        pack,
        out_shape=shape((atoms + POS_ROWS, channels), bf16),
        in_specs=hbm(2),
        out_specs=pl.BlockSpec(memory_space=pltpu.VMEM),
        scratch_shapes=[pltpu.VMEM((3, atoms), bf16), pltpu.SemaphoreType.DMA((2,))],
        name="pack",
        compiler_params=grant(2),
    )(*in_hbm(feats, positions))
    x_out = lax.ppermute(own, "gx", pair_out("gx"))
    x_in = lax.ppermute(own, "gx", pair_in("gx"))

    slab = pl.pallas_call(
        assemble,
        out_shape=shape((3 * (atoms + POS_ROWS), channels), bf16),
        in_specs=vmem(3),
        out_specs=pl.BlockSpec(memory_space=pltpu.VMEM),
        name="assemble",
        compiler_params=grant(2),
    )(own, x_out, x_in)
    y_out = lax.ppermute(slab, "gy", pair_out("gy"))
    y_in = lax.ppermute(slab, "gy", pair_in("gy"))

    *prepared, w2_copy, we_copy, rows_own, pos_own = pl.pallas_call(
        prepare,
        out_shape=[
            shape((edges, 9 * atoms), bf16),
            shape((edges, atoms), bf16),
            shape((edges, edges), bf16),
            shape((channels, edges), f32),
            shape((16, edges), f32),
            shape((channels, channels), bf16),
            shape((channels, channels), bf16),
            shape((3 * channels, channels), bf16),
            shape((channels, 4 * NBASIS), bf16),
            shape((2 * NBASIS, channels), bf16),
            shape((3, channels, edges), f32),
            shape((channels, channels), bf16),
            shape((channels, 3 * channels), bf16),
            shape((edges, channels), f32),
            shape((8, edges), f32),
        ],
        in_specs=vmem(1) + hbm(12),
        out_specs=vmem(15),
        scratch_shapes=[
            pltpu.VMEM(part.shape, part.dtype)
            for part in (
                feats,
                positions,
                atom_count,
                edge_center,
                edge_neighbor,
                edge_valid,
                w_center,
                w_neighbor,
                w_radial,
                readout,
            )
        ]
        + [pltpu.SemaphoreType.DMA((12,))],
        name="prepare",
        compiler_params=grant(8),
        cost_estimate=pl.CostEstimate(flops=100000000, bytes_accessed=3000000, transcendentals=0),
    )(
        slab,
        *in_hbm(
            feats,
            positions,
            atom_count,
            edge_center,
            edge_neighbor,
            edge_valid,
            w_center,
            w_neighbor,
            w_radial,
            w_second,
            w_env,
            readout,
        )
    )

    f_own, f_in, f_out = pl.pallas_call(
        layer,
        out_shape=[shape((4, 3 * atoms), f32)] + [shape((3, 3 * atoms), f32)] * 2,
        in_specs=vmem(17),
        out_specs=vmem(3),
        name="layer",
        compiler_params=grant(8),
    )(y_in, y_out, *prepared, w2_copy, we_copy, rows_own, pos_own)

    r_out = lax.ppermute(f_out, "gy", pair_out("gy"))
    r_in = lax.ppermute(f_in, "gy", pair_in("gy"))
    column = f_own[0:3] + r_out + r_in
    energy = f_own[3:4, :atoms][None]
    s_up = lax.ppermute(column[:, atoms : 2 * atoms], "gx", step_by("gx", 1))
    s_down = lax.ppermute(column[:, 2 * atoms :], "gx", step_by("gx", -1))
    forces = column[:, :atoms] + s_up + s_down
    return (energy, forces[None, None])


def solution(mesh):
    return jax.shard_map(
        body,
        mesh=mesh,
        in_specs=(
            P("gx", "gy", None, None),
            P("gx", "gy", None, None),
            P(),
            P("gx", "gy", None),
            P("gx", "gy", None),
            P("gx", "gy", None),
            P(),
            P(),
            P(),
            P(),
            P(),
            P(),
        ),
        out_specs=(P("gx", "gy", None), P("gx", "gy", None, None)),
        check_vma=False,
    )
```

```python
import math

import jax
import jax.numpy as jnp
from jax import lax
from jax.experimental import pallas as pl
from jax.experimental.pallas import tpu as pltpu
from jax.sharding import PartitionSpec as P

NBASIS = 8
EBLK = 64
POS_ROWS = 16

ROOT_THREE = math.sqrt(3.0)
ROOT_FIFTEEN = math.sqrt(15.0)
ROOT_FIVE = math.sqrt(5.0)
GAMMAS = [0.25 * 1.5**k for k in range(NBASIS)]

NN = (((1,), (0,)), ((), ()))
NT = (((1,), (1,)), ((), ()))


def mm(a, b, dims=NN):
    return lax.dot_general(a, b, dims, preferred_element_type=jnp.float32)


def turned(w):
    return w.astype(jnp.float32).T


def halves(x):
    high = x.astype(jnp.bfloat16).astype(jnp.float32)
    return high, x - high


def prepare(
    slab,
    feats_hbm,
    positions_hbm,
    count_hbm,
    center_hbm,
    neighbor_hbm,
    valid_hbm,
    w_center_hbm,
    w_neighbor_hbm,
    w_radial_hbm,
    w_second_hbm,
    w_env_hbm,
    readout_hbm,
    hot_nb,
    hot_c,
    same,
    near,
    aux,
    wn_t,
    w2_t,
    we_t,
    wr_t,
    wr16,
    read_b,
    w2_copy,
    we_copy,
    rows_own,
    pos_own,
    feats,
    positions,
    atom_count,
    center,
    neighbor,
    valid,
    w_center,
    w_neighbor,
    w_radial,
    readout,
    sems,
):
    moves = [
        pltpu.make_async_copy(source, target, sems.at[k])
        for k, (source, target) in enumerate(
            (
                (neighbor_hbm, neighbor),
                (center_hbm, center),
                (valid_hbm, valid),
                (count_hbm, atom_count),
                (feats_hbm, feats),
                (positions_hbm, positions),
                (w_center_hbm, w_center),
                (w_neighbor_hbm, w_neighbor),
                (w_second_hbm, w2_copy),
                (w_env_hbm, we_copy),
                (w_radial_hbm, w_radial),
                (readout_hbm, readout),
            )
        )
    ]
    for move in moves:
        move.start()
    atoms = feats.shape[2]
    edges = center.shape[2]
    gx, gy = lax.axis_index("gx"), lax.axis_index("gy")
    for move in moves[:4]:
        move.wait()
    c_row = center[0]
    n_row = neighbor[0]
    slot = n_row // atoms
    atom = n_row - slot * atoms
    row_a = jnp.where(slot >= 3, 1, 0) + jnp.where(slot >= 6, 1, 0)
    row_b = slot - 3 * row_a
    in_a = 2 - 2 * (gx % 2)
    in_b = 2 - 2 * (gy % 2)
    place_x = jnp.where(row_a == 1, 0, jnp.where(row_a == in_a, 1, 2))
    place_y = jnp.where(row_b == 1, 0, jnp.where(row_b == in_b, 1, 2))
    local = (3 * place_y + place_x) * atoms + atom
    stacked = jnp.concatenate(
        [
            jnp.broadcast_to(local.astype(jnp.float32), (8, edges)),
            jnp.broadcast_to(c_row.astype(jnp.float32), (8, edges)),
        ],
        axis=0,
    ).T
    n_col = stacked[:, 0:1].astype(jnp.int32)
    c_col = stacked[:, 8:9].astype(jnp.int32)
    lane = lax.broadcasted_iota(jnp.int32, (edges, atoms), 1)
    for part in range(9):
        hot_nb[:, part * atoms : (part + 1) * atoms] = jnp.where(
            lane == n_col - part * atoms, 1.0, 0.0
        ).astype(jnp.bfloat16)
    wide = 3 * atoms
    hot = hot_nb[:, 0:wide]
    rows_own[...] = mm(hot, slab[0:wide])
    packed = slab[wide : wide + 3 * POS_ROWS].astype(jnp.float32)
    pos = jnp.concatenate([packed[8 * k : 8 * k + 8] for k in range(6)], axis=1)
    pos = jnp.concatenate([pos, jnp.zeros_like(pos)], axis=0).astype(jnp.bfloat16)
    pos_own[...] = mm(pos, hot, NT)[0:8]
    c_hot = jnp.where(lane == c_col, 1.0, 0.0).astype(jnp.bfloat16)
    hot_c[...] = c_hot
    same[...] = jnp.where(c_col == c_row, 1.0, 0.0).astype(jnp.bfloat16)

    for move in moves[4:]:
        move.wait()
    near_all = mm(feats[0, 0], w_center[...]).astype(jnp.bfloat16)
    near[...] = mm(c_hot, near_all).T
    pos16 = jnp.concatenate(
        [positions[0, 0].astype(jnp.float32), jnp.zeros((13, atoms), jnp.float32)], axis=0
    ).astype(jnp.bfloat16)
    pos_c = mm(pos16, c_hot, NT)
    here = (lax.broadcasted_iota(jnp.int32, atom_count.shape, 0) == gx) & (
        lax.broadcasted_iota(jnp.int32, atom_count.shape, 1) == gy
    )
    count = jnp.where(here, atom_count[...], 0).astype(jnp.float32)
    count = jnp.sum(jnp.sum(count, axis=1, keepdims=True), axis=0, keepdims=True)
    used = (count.astype(jnp.int32) * (edges // EBLK) + atoms - 1) // atoms
    block = lax.broadcasted_iota(jnp.int32, (1, edges), 1) // EBLK
    mask = jnp.where(block < used, valid[0], 0).astype(jnp.float32)
    aux[...] = jnp.concatenate(
        [
            (row_a - 1).astype(jnp.float32),
            (row_b - 1).astype(jnp.float32),
            jnp.zeros((1, edges), jnp.float32),
            mask,
            jnp.zeros((4, edges), jnp.float32),
            pos_c[0:8],
        ],
        axis=0,
    )

    wn_t[...] = turned(w_neighbor[...]).astype(jnp.bfloat16)
    w2_t[...] = turned(w2_copy[...]).astype(jnp.bfloat16)
    we_t[...] = turned(we_copy[...]).astype(jnp.bfloat16)
    high, low = halves(w_radial[...])
    wr16[...] = jnp.concatenate([high, low], axis=0).astype(jnp.bfloat16)
    wr_t[...] = (
        jnp.concatenate([high, high, low, jnp.zeros_like(high)], axis=0).T.astype(jnp.bfloat16)
    )
    channels = w_center.shape[0]
    read_t = jnp.concatenate(
        [readout[...], jnp.zeros((5, channels), jnp.float32)], axis=0
    ).T
    for level in range(3):
        read_b[level] = jnp.broadcast_to(read_t[:, level : level + 1], (channels, edges))


def layer(
    slab_in,
    slab_out,
    hot_nb,
    hot_c,
    same,
    near,
    aux,
    wn_t,
    w2_t,
    we_t,
    wr_t,
    wr16,
    read_b,
    w_second,
    w_env,
    rows_own,
    pos_own,
    f_own,
    f_in,
    f_out,
):
    bf16, f32 = jnp.bfloat16, jnp.float32
    channels, edges = near.shape
    atoms = hot_c.shape[1]
    wide = 3 * atoms
    rows_nb = rows_own[...]
    pos_nb = pos_own[...]
    for part, slab in enumerate((slab_in, slab_out), 1):
        hot = hot_nb[:, part * wide : (part + 1) * wide]
        rows_nb = rows_nb + mm(hot, slab[0:wide])
        packed = slab[wide : wide + 3 * POS_ROWS].astype(f32)
        pos = jnp.concatenate([packed[8 * k : 8 * k + 8] for k in range(6)], axis=1)
        pos = jnp.concatenate([pos, jnp.zeros_like(pos)], axis=0).astype(bf16)
        pos_nb = pos_nb + mm(pos, hot, NT)[0:8]
    far = mm(wn_t[...], rows_nb.astype(bf16), NT).astype(bf16).astype(f32)

    mask = aux[3:4]
    d = pos_nb[0:3] + aux[0:3] - aux[8:11]
    dist_sq = jnp.sum(d * d, axis=0, keepdims=True) + 0.25
    inv = lax.rsqrt(dist_sq)
    dist = jnp.sqrt(dist_sq)
    u = d / dist
    ux, uy, uz = u[0:1], u[1:2], u[2:3]
    sub = lax.broadcasted_iota(jnp.int32, (NBASIS, edges), 0)
    gamma = jnp.full((NBASIS, edges), GAMMAS[0], f32)
    for k in range(1, NBASIS):
        gamma = jnp.where(sub == k, GAMMAS[k], gamma)
    basis = jnp.exp(-gamma * dist_sq)
    b_high, b_low = halves(basis)
    b32 = jnp.concatenate([b_high, b_low, b_high, jnp.zeros_like(b_high)], axis=0).astype(bf16)
    radial = mm(wr_t[...], b32)
    pre = (near[...] + far + radial).astype(bf16).astype(f32)
    sig = jax.nn.sigmoid(pre)
    latent = jnp.tanh(mm(w2_t[...], (pre * sig).astype(bf16))).astype(bf16)
    env = mm(we_t[...], latent) * mask
    harm = [
        None,
        ROOT_THREE * ux,
        ROOT_THREE * uy,
        ROOT_THREE * uz,
        ROOT_FIFTEEN * ux * uy,
        ROOT_FIFTEEN * uy * uz,
        0.5 * ROOT_FIVE * (3.0 * uz * uz - 1.0),
        ROOT_FIFTEEN * ux * uz,
        0.5 * ROOT_FIFTEEN * (ux * ux - uy * uy),
    ]
    term = jnp.sum(read_b[0] * env[0:channels], axis=0, keepdims=True)
    grads = [read_b[0] * mask]
    hg = [None] * 9
    for level, comps in ((1, (1, 2, 3)), (2, (4, 5, 6, 7, 8))):
        part = env[level * channels : (level + 1) * channels]
        twice = 2.0 * read_b[level]
        scaled = twice * part
        total = jnp.zeros((channels, edges), f32)
        for m in comps:
            gathered = mm((part * harm[m]).astype(bf16), same[...])
            hg[m] = jnp.sum(gathered * scaled, axis=0, keepdims=True)
            total = total + gathered * harm[m]
            term = term + 0.5 * harm[m] * hg[m]
        grads.append(twice * total * mask)
    env_grad = jnp.concatenate(grads, axis=0).astype(bf16)
    lat = latent.astype(f32)
    act_grad = (mm(w_env[...], env_grad) * (1.0 - lat * lat)).astype(bf16)
    pre_grad = mm(w_second[...], act_grad) * sig * (1.0 + pre * (1.0 - sig))
    p_high, p_low = halves(pre_grad)
    both = mm(wr16[...], p_high.astype(bf16)) + mm(wr16[...], p_low.astype(bf16))
    basis_grad = both[0:NBASIS] + both[NBASIS : 2 * NBASIS]
    ds = -jnp.sum(gamma * basis * basis_grad, axis=0, keepdims=True)
    gx = ROOT_THREE * hg[1] + ROOT_FIFTEEN * (uy * hg[4] + uz * hg[7] + ux * hg[8])
    gy = ROOT_THREE * hg[2] + ROOT_FIFTEEN * (ux * hg[4] + uz * hg[5] - uy * hg[8])
    gz = ROOT_THREE * hg[3] + ROOT_FIFTEEN * (uy * hg[5] + ux * hg[7]) + 3.0 * ROOT_FIVE * uz * hg[6]
    ds = ds - 0.5 * inv * inv * (gx * ux + gy * uy + gz * uz)
    g = jnp.concatenate([gx, gy, gz], axis=0)
    dg = g * inv + 2.0 * d * ds
    four_high, four_low = halves(jnp.concatenate([dg, term], axis=0))
    lines = jnp.concatenate([four_high, four_low, jnp.zeros((8, edges), f32)], axis=0).astype(bf16)
    to_c = mm(lines, hot_c[...])
    to_c = to_c[0:4] + to_c[4:8]
    f_own[3:4, 0:atoms] = to_c[3:4]
    f_own[3:4, atoms:wide] = jnp.zeros((1, wide - atoms), f32)
    for part, out in enumerate((f_own, f_in, f_out)):
        to_nb = mm(lines, hot_nb[:, part * wide : (part + 1) * wide])
        to_nb = -(to_nb[0:3] + to_nb[4:7])
        mine, inner, outer = (to_nb[:, k * atoms : (k + 1) * atoms] for k in range(3))
        out[0:3, 0:atoms] = mine + to_c[0:3] if part == 0 else mine
        out[0:3, atoms : 2 * atoms] = inner
        out[0:3, 2 * atoms : wide] = outer


def pack(feats, positions, packed, pos, sems):
    atoms = feats.shape[2]
    half = atoms // 2
    move_pos = pltpu.make_async_copy(positions.at[0, 0], pos, sems.at[0])
    move_feats = pltpu.make_async_copy(feats.at[0, 0], packed.at[0:atoms], sems.at[1])
    move_pos.start()
    move_feats.start()
    move_pos.wait()
    rows = pos[...].astype(jnp.float32)
    gap = jnp.zeros((5, half), jnp.float32)
    packed[atoms : atoms + POS_ROWS] = jnp.concatenate(
        [rows[:, :half], gap, rows[:, half:], gap], axis=0
    ).astype(jnp.bfloat16)
    move_feats.wait()


def assemble(own, x_out, x_in, slab):
    atoms = own.shape[0] - POS_ROWS
    for k, part in enumerate((own, x_in, x_out)):
        slab[k * atoms : (k + 1) * atoms] = part[0:atoms]
        start = 3 * atoms + k * POS_ROWS
        slab[start : start + POS_ROWS] = part[atoms : atoms + POS_ROWS]


def grant(mib):
    return pltpu.CompilerParams(vmem_limit_bytes=mib << 20)


def vmem(n):
    return [pl.BlockSpec(memory_space=pltpu.VMEM)] * n


def in_hbm(*arrays):
    return [pltpu.with_memory_space_constraint(a, pltpu.HBM) for a in arrays]


def hbm(n):
    return [pl.BlockSpec(memory_space=pltpu.HBM)] * n


def pair_in(axis):
    return [(i, i ^ 1) for i in range(lax.axis_size(axis))]


def pair_out(axis):
    count = lax.axis_size(axis)
    return [(i, (i + 1) % count if i % 2 else (i - 1) % count) for i in range(count)]


def body(
    feats,
    positions,
    atom_count,
    edge_center,
    edge_neighbor,
    edge_valid,
    w_center,
    w_neighbor,
    w_radial,
    w_second,
    w_env,
    readout,
):
    f32, bf16 = jnp.float32, jnp.bfloat16
    atoms, channels = feats.shape[2:]
    edges = edge_center.shape[2]
    shape = jax.ShapeDtypeStruct
    own = pl.pallas_call(
        pack,
        out_shape=shape((atoms + POS_ROWS, channels), bf16),
        in_specs=hbm(2),
        out_specs=pl.BlockSpec(memory_space=pltpu.VMEM),
        scratch_shapes=[pltpu.VMEM((3, atoms), bf16), pltpu.SemaphoreType.DMA((2,))],
        name="pack",
        compiler_params=grant(2),
    )(*in_hbm(feats, positions))
    x_out = lax.ppermute(own, "gx", pair_out("gx"))
    x_in = lax.ppermute(own, "gx", pair_in("gx"))

    slab = pl.pallas_call(
        assemble,
        out_shape=shape((3 * (atoms + POS_ROWS), channels), bf16),
        in_specs=vmem(3),
        out_specs=pl.BlockSpec(memory_space=pltpu.VMEM),
        name="assemble",
        compiler_params=grant(2),
    )(own, x_out, x_in)
    y_out = lax.ppermute(slab, "gy", pair_out("gy"))
    y_in = lax.ppermute(slab, "gy", pair_in("gy"))

    *prepared, w2_copy, we_copy, rows_own, pos_own = pl.pallas_call(
        prepare,
        out_shape=[
            shape((edges, 9 * atoms), bf16),
            shape((edges, atoms), bf16),
            shape((edges, edges), bf16),
            shape((channels, edges), f32),
            shape((16, edges), f32),
            shape((channels, channels), bf16),
            shape((channels, channels), bf16),
            shape((3 * channels, channels), bf16),
            shape((channels, 4 * NBASIS), bf16),
            shape((2 * NBASIS, channels), bf16),
            shape((3, channels, edges), f32),
            shape((channels, channels), bf16),
            shape((channels, 3 * channels), bf16),
            shape((edges, channels), f32),
            shape((8, edges), f32),
        ],
        in_specs=vmem(1) + hbm(12),
        out_specs=vmem(15),
        scratch_shapes=[
            pltpu.VMEM(part.shape, part.dtype)
            for part in (
                feats,
                positions,
                atom_count,
                edge_center,
                edge_neighbor,
                edge_valid,
                w_center,
                w_neighbor,
                w_radial,
                readout,
            )
        ]
        + [pltpu.SemaphoreType.DMA((12,))],
        name="prepare",
        compiler_params=grant(8),
        cost_estimate=pl.CostEstimate(flops=100000000, bytes_accessed=3000000, transcendentals=0),
    )(
        slab,
        *in_hbm(
            feats,
            positions,
            atom_count,
            edge_center,
            edge_neighbor,
            edge_valid,
            w_center,
            w_neighbor,
            w_radial,
            w_second,
            w_env,
            readout,
        )
    )

    f_own, f_in, f_out = pl.pallas_call(
        layer,
        out_shape=[shape((4, 3 * atoms), f32)] + [shape((3, 3 * atoms), f32)] * 2,
        in_specs=vmem(17),
        out_specs=vmem(3),
        name="layer",
        compiler_params=grant(8),
    )(y_in, y_out, *prepared, w2_copy, we_copy, rows_own, pos_own)

    r_out = lax.ppermute(f_out, "gy", pair_out("gy"))
    r_in = lax.ppermute(f_in, "gy", pair_in("gy"))
    column = f_own[0:3] + r_out + r_in
    energy = f_own[3:4, :atoms][None]
    s_in = lax.ppermute(column[:, atoms : 2 * atoms], "gx", pair_in("gx"))
    s_out = lax.ppermute(column[:, 2 * atoms :], "gx", pair_out("gx"))
    forces = column[:, :atoms] + s_out + s_in
    return (energy, forces[None, None])


def solution(mesh):
    return jax.shard_map(
        body,
        mesh=mesh,
        in_specs=(
            P("gx", "gy", None, None),
            P("gx", "gy", None, None),
            P(),
            P("gx", "gy", None),
            P("gx", "gy", None),
            P("gx", "gy", None),
            P(),
            P(),
            P(),
            P(),
            P(),
            P(),
        ),
        out_specs=(P("gx", "gy", None), P("gx", "gy", None, None)),
        check_vma=False,
    )
```
